128 devices in a mesh: seq: 8 (over y_hi, z), fsdp: 16 (over y_lo, x, core).
Axes of the slice: x: 4, y: 4 (y_hi: 2, y_lo: 2; y = y_hi * 2 + y_lo), z: 4, core: 2. Of those that a mesh axis runs over, the one named last changes fastest.
Arguments:
- signal: bfloat16 [16, 1024, 8192], P('fsdp', 'seq'), may hold values from -6 to 6
- gating: bfloat16 [16, 1024, 8192], P('fsdp', 'seq'), may hold values from -6 to 6
- low_rank: bfloat16 [16, 1024, 512], P('fsdp', 'seq'), may hold values from -6 to 6
- dt_weight: bfloat16 [512, 8192], P(None, 'fsdp'), may hold values from -0.25 to 0.25
- dt_bias: float32 [8192], P('fsdp'), may hold values from -1 to 0.5
- decay_rate: float32 [16, 8192], P(None, 'fsdp'), may hold values from 0 to 0.05, as said below
- skip_gain: float32 [8192], P('fsdp'), may hold values from 0.5 to 1.5
- coef_in: float32 [16, 16, 1024], P('fsdp', None, 'seq'), may hold values from -4 to 4
- coef_out: float32 [16, 16, 1024], P('fsdp', None, 'seq'), may hold values from -0.1875 to 0.1875
- segment_ids: int32 [16, 1024], P('fsdp', 'seq'), may hold values from 0 to 3, never falling along the last dimension, each value on 1 to 512 neighbouring positions
- out_grad: bfloat16 [16, 1024, 8192], P('fsdp', 'seq'), may hold values from -6 to 6
Outputs:
- grad_signal: bfloat16 [16, 1024, 8192], P('fsdp', 'seq')
- grad_gating: bfloat16 [16, 1024, 8192], P('fsdp', 'seq')
- grad_low_rank: float32 [16, 1024, 512], P('fsdp', 'seq')
- grad_coef_in: float32 [16, 16, 1024], P('fsdp', None, 'seq')
- grad_coef_out: float32 [16, 16, 1024], P('fsdp', None, 'seq')
- grad_dt_weight: float32 [512, 8192], P(None, 'fsdp')
- grad_rate: float32 [16, 8192], P(None, 'fsdp')
- grad_skip: float32 [8192], P('fsdp')
- grad_bias: float32 [8192], P('fsdp')
The draws below stay inside these ranges and needn't reach their ends.
Inputs may be any that keep to these rules, and one draw needn't show every extreme that they name: `segment_ids`: segment numbers never fall along a sequence; each document is a run of one number. `decay_rate`: positive rates.
All inputs are finite; a program needn't handle non-finite values.
Results may differ from the reference program's by a relative error of at most 0.0029.
Values may be sent and summed in bfloat16 or wider, within the bound.
A program may use at most 192 MiB of HBM per device.

```python
import math
import jax
import jax.numpy as jnp
import numpy as np
from jax import lax

E = 8192
N = 16
R = 512
SEQLEN = 1024
BATCH = 16


def draw_decay_rate(key, part):
    first, second, third = jax.random.split(key, 3)
    share = 0.5
    slow_mask = jax.random.uniform(first, (N, E), jnp.float32) < share
    slow_rate = jnp.exp(jax.random.uniform(second, (N, E), jnp.float32, jnp.log(0.1), jnp.log(1.0))) / SEQLEN
    fast_rate = jnp.exp(jax.random.uniform(third, (N, E), jnp.float32, jnp.log(0.02), jnp.log(0.05)))
    return jnp.where(slow_mask, slow_rate, fast_rate).astype(jnp.float32)


def steps_of(rng, shape, pieces, smallest, top_value):
    def one(dim, blocks):
        steps = jax.random.uniform(jax.random.fold_in(jax.random.fold_in(rng, 6), dim), (blocks,), jnp.float32, smallest / len(pieces), top_value / len(pieces))
        return jnp.repeat(jnp.exp(steps), shape[dim] // blocks).reshape((-1,) + (1,) * (len(shape) - dim - 1))

    gain = one(*pieces[0])
    for cut in pieces[1:]:
        gain = gain * one(*cut)
    return gain


def profile(number_of, total, most, slope):
    portions = [(1 << 20) // math.isqrt(rank ** slope) + 1 for rank in range(2, number_of + 1)]
    surplus, counts = total - most - (number_of - 1), [1] * (number_of - 1)
    while surplus > 0:
        free = [i for i in range(number_of - 1) if counts[i] < most]
        pool, left = sum([portions[i] for i in free]), surplus
        for i in free:
            addition = min(most - counts[i], max(1, left * portions[i] // pool), surplus)
            counts[i] = counts[i] + addition
            surplus = surplus - addition
    return np.array([most] + counts)


def ragged(own_key, number_of, total, reach, lean):
    if number_of == 2:
        one = jax.random.randint(own_key, (), max(1, total - reach), min(reach, total - 1) + 1)
        return jnp.stack([one, total - one])
    tallies = jnp.asarray(profile(number_of, total, reach, lean), jnp.int32)
    couples = (number_of - 1) // 2
    source_of, taker = tallies[1:1 + 2 * couples:2], tallies[2:2 + 2 * couples:2]
    room = jnp.minimum(source_of - 1, reach - taker)
    passed = jax.random.randint(jax.random.fold_in(own_key, 1), (couples,), 0, 1 << 20) % (room + 1)
    tallies = tallies.at[1:1 + 2 * couples:2].set(source_of - passed).at[2:2 + 2 * couples:2].set(taker + passed)
    return tallies[jax.random.permutation(jax.random.fold_in(own_key, 2), number_of)]


def noise(rng, extent, scale, reach, cuts=(), kind=jnp.bfloat16):
    array = scale * jax.random.normal(rng, extent, jnp.float32)
    if cuts:
        array = array * steps_of(rng, extent, cuts, -0.22, 0.18)
    return jnp.clip(array, -reach, reach).astype(kind)


def setup_inputs(seed: int = 0) -> dict:
    streams_of = jax.random.split(jax.random.key(seed), 12)
    signal = noise(streams_of[0], (BATCH, SEQLEN, E), 1.0, 6.0, ((0, 16), (1, 8)))
    gating = noise(streams_of[1], (BATCH, SEQLEN, E), 1.0, 6.0, ((0, 16), (1, 8)))
    low_rank = noise(streams_of[2], (BATCH, SEQLEN, R), 1.0, 6.0, ((0, 16), (1, 8)))
    dt_weight = noise(streams_of[3], (R, E), R ** -0.5, 0.25, ((1, 16),))
    dt_bias = jnp.clip(-1.0 + 1.5 * jax.random.uniform(streams_of[4], (E,), jnp.float32) ** steps_of(streams_of[4], (E,), ((0, 16),), -0.2, 0.2), -1.0, 0.5)
    decay_rate = draw_decay_rate(jax.random.fold_in(streams_of[11], 71), 0)
    skip_gain = jnp.clip(0.5 + 1.0 * jax.random.uniform(streams_of[6], (E,), jnp.float32) ** steps_of(streams_of[6], (E,), ((0, 16),), -0.2, 0.2), 0.5, 1.5)
    coef_in = noise(streams_of[7], (BATCH, N, SEQLEN), 0.5, 4.0, ((0, 16), (2, 8)), jnp.float32)
    coef_out = noise(streams_of[8], (BATCH, N, SEQLEN), (1.0 / SEQLEN ** 0.5), 0.1875, ((0, 16), (2, 8)), jnp.float32)
    segment_ids = jax.vmap(lambda own: jnp.searchsorted(jnp.cumsum(ragged(own, 4, SEQLEN, SEQLEN // 2, 0)), jnp.arange(SEQLEN), side="right"))(jax.random.split(streams_of[9], BATCH)).reshape((BATCH, SEQLEN)).astype(jnp.int32)
    out_grad = noise(streams_of[10], (BATCH, SEQLEN, E), 1.0, 6.0, ((0, 16), (1, 8)))
    return {"signal": signal, "gating": gating, "low_rank": low_rank, "dt_weight": dt_weight, "dt_bias": dt_bias, "decay_rate": decay_rate, "skip_gain": skip_gain, "coef_in": coef_in, "coef_out": coef_out, "segment_ids": segment_ids, "out_grad": out_grad}


def one_sequence(items, dt_weight, dt_bias, decay_rate, skip_gain):
    signal, gating, low_rows, coef_in, coef_out, seg_row, out_grad = items
    sig_f = signal.astype(jnp.float32)
    gate_f = gating.astype(jnp.float32)
    cot_f = out_grad.astype(jnp.float32)
    dt_raw = jnp.dot(low_rows, dt_weight, preferred_element_type=jnp.float32) + dt_bias[None, :]
    delta = jax.nn.softplus(dt_raw)
    keep = jnp.concatenate([jnp.zeros((1,), jnp.float32), (seg_row[1:] == seg_row[:-1]).astype(jnp.float32)])
    zeros_state = jnp.zeros(decay_rate.shape, jnp.float32)

    def forward_step(state, row):
        d_row, k_val, s_row, b_col = row
        decay = jnp.exp(-d_row[None, :] * decay_rate) * k_val
        state = decay * state + (d_row * s_row)[None, :] * b_col[:, None]
        return state, state

    _, history = lax.scan(forward_step, zeros_state, (delta, keep, sig_f, coef_in.T))
    scan_out = jnp.sum(coef_out.T[:, :, None] * history, 1) + skip_gain[None, :] * sig_f
    sig_gate = jax.nn.sigmoid(gate_f)
    out_adj = cot_f * gate_f * sig_gate
    gate_grad = cot_f * scan_out * sig_gate * (1.0 + gate_f * (1.0 - sig_gate))
    prior = jnp.concatenate([jnp.zeros((1,) + decay_rate.shape, jnp.float32), history[:-1]], 0)

    def backward_step(running, row):
        carried, rate_grad = running
        d_row, k_val, s_row, b_col, c_col, a_row, p_state = row
        decay = jnp.exp(-d_row[None, :] * decay_rate) * k_val
        adj = c_col[:, None] * a_row[None, :] + carried
        in_grad = jnp.sum(adj * (d_row * s_row)[None, :], 1)
        sig_grad = d_row * jnp.sum(adj * b_col[:, None], 0) + skip_gain * a_row
        delta_grad = jnp.sum(adj * (b_col[:, None] * s_row[None, :] - decay_rate * decay * p_state), 0)
        rate_grad = rate_grad - adj * p_state * decay * d_row[None, :]
        return (decay * adj, rate_grad), (in_grad, sig_grad, delta_grad)

    (_, rate_grad), (in_grad, sig_grad, delta_grad) = lax.scan(
        backward_step, (zeros_state, zeros_state),
        (delta, keep, sig_f, coef_in.T, coef_out.T, out_adj, prior), reverse=True)
    out_coef_grad = jnp.sum(history * out_adj[:, None, :], 2)
    raw_grad = delta_grad * jax.nn.sigmoid(dt_raw)
    raw_rounded = raw_grad.astype(jnp.bfloat16)
    low_grad = lax.dot_general(raw_rounded, dt_weight, (((1,), (1,)), ((), ())), preferred_element_type=jnp.float32)
    weight_part = lax.dot_general(low_rows, raw_rounded, (((0,), (0,)), ((), ())), preferred_element_type=jnp.float32)
    skip_part = jnp.sum(sig_f * out_adj, 0)
    bias_part = jnp.sum(raw_grad, 0)
    return (sig_grad.astype(jnp.bfloat16), gate_grad.astype(jnp.bfloat16), low_grad, in_grad.T, out_coef_grad.T,
            weight_part, rate_grad, skip_part, bias_part)


def reference(signal, gating, low_rank, dt_weight, dt_bias, decay_rate, skip_gain, coef_in, coef_out, segment_ids, out_grad):
    def single(items):
        return one_sequence(items, dt_weight, dt_bias, decay_rate, skip_gain)

    results = lax.map(single, (signal, gating, low_rank, coef_in, coef_out, segment_ids, out_grad))
    return (results[0], results[1], results[2], results[3], results[4],
            jnp.sum(results[5], 0), jnp.sum(results[6], 0), jnp.sum(results[7], 0), jnp.sum(results[8], 0))
```

```python
import functools, math
import jax, jax.numpy as jnp
from jax import lax
from jax.experimental import pallas as pl
from jax.experimental.pallas import tpu as pltpu
from jax.sharding import PartitionSpec as P

F32, BF16 = jnp.float32, jnp.bfloat16
LANES = 128
SUB = 16
LOG2E = math.log2(math.e)

def lanes(g):
    return slice(g * LANES, (g + 1) * LANES)

def prepare(low, w, bias, sig, gate, cot, keep):
    raw = jnp.dot(low, w, preferred_element_type=F32) + bias
    delta = jnp.maximum(raw, 0.0) + jnp.log1p(jnp.exp(-jnp.abs(raw)))
    s = sig.astype(F32)
    g = gate.astype(F32)
    sg = jax.nn.sigmoid(g)
    a = cot.astype(F32) * g * sg
    ks = jnp.concatenate([keep] * (raw.shape[1] // LANES), 1)
    dk = jnp.where(ks > 0, delta, jnp.inf)
    return raw, delta, dk, delta * s, a

def local_kernel(low, w, bias, rate, sig, gate, cot, keep, inb, outb, end, back, total, dk_s, ds_s, a_s):
    tokens, width = sig.shape
    groups = width // LANES
    raw, delta, dk, ds, a = prepare(low[...], w[...], bias[...], sig[...], gate[...], cot[...], keep[...])
    dk_s[...] = dk
    ds_s[...] = ds
    a_s[...] = a
    total[...] = jnp.sum(dk, 0, keepdims=True)
    states = rate.shape[0]
    nrate = [rate[:, lanes(g)] * (-LOG2E) for g in range(groups)]
    def body(i, carry):
        st, ad = list(carry[0]), list(carry[1])
        fb = pl.ds(pl.multiple_of(i * SUB, SUB), SUB)
        rb = pl.ds(pl.multiple_of(tokens - SUB - i * SUB, SUB), SUB)
        for u in range(SUB):
            t = i * SUB + u
            v = tokens - 1 - t
            bb = inb[pl.ds(pl.multiple_of(t * states, states), states), :]
            cc = outb[pl.ds(pl.multiple_of(v * states, states), states), :]
            for g in range(groups):
                dec = jnp.exp2(nrate[g] * dk_s.at[fb, lanes(g)][u:u + 1, :])
                st[g] = dec * st[g] + bb * ds_s.at[fb, lanes(g)][u:u + 1, :]
                dec2 = jnp.exp2(nrate[g] * dk_s.at[rb, lanes(g)][SUB - 1 - u:SUB - u, :])
                ad[g] = dec2 * (cc * a_s.at[rb, lanes(g)][SUB - 1 - u:SUB - u, :] + ad[g])
        return tuple(st), tuple(ad)
    z = tuple(jnp.zeros((states, LANES), F32) for _ in range(groups))
    st, ad = lax.fori_loop(0, tokens // SUB, body, (z, z))
    for g in range(groups):
        end[:, lanes(g)] = st[g]
        back[:, lanes(g)] = ad[g]

def full_kernel(low, w, bias, rate, skip, sig, gate, cot, keep, inb, outb, cmat, bmat, omat, s_in, a_in,
                g_sig, g_gate, g_low, g_inc, g_outc, dw, g_rate, g_skip, g_bias,
                dk_s, d_s, ds_s, a_s, r_s, hist, dec_s, hb0, hb1, ab0, ab1, al0, al1, zr0, zr1,
                ascan, ab16, db16, q_s, zz_s, oc_s, ic_s, *, lo):
    step = pl.program_id(0)
    tokens, width = sig.shape
    groups = width // LANES
    states = rate.shape[0]
    blk = SUB * states
    nblk = tokens // SUB
    raw, delta, dk, ds, a = prepare(low[...], w[...], bias[...], sig[...], gate[...], cot[...], keep[...])
    dk_s[...] = dk
    d_s[...] = delta
    ds_s[...] = ds
    a_s[...] = a
    r_s[...] = jax.nn.sigmoid(raw)

    def split(ref, x):
        hi = x.astype(BF16)
        lowp = (x - hi.astype(F32)).astype(BF16)
        for k in range(nblk):
            ref[2 * SUB * (k + 1):2 * SUB * (k + 1) + SUB, :] = hi[k * SUB:(k + 1) * SUB]
            ref[2 * SUB * (k + 1) + SUB:2 * SUB * (k + 2), :] = lowp[k * SUB:(k + 1) * SUB]
    split(ab16, a)
    split(db16, ds)

    @pl.when(step == 0)
    def _():
        oc_s[...] = jnp.zeros_like(oc_s)
        ic_s[...] = jnp.zeros_like(ic_s)
        g_low[...] = jnp.zeros_like(g_low)

    nrate = [rate[:, lanes(g)] * (-LOG2E) for g in range(groups)]
    st0 = tuple(s_in[:, lanes(g)] for g in range(groups))
    for g in range(groups):
        hist[0:states, lanes(g)] = st0[g]

    def nt(x, y):
        return lax.dot_general(x, y, (((1,), (1,)), ((), ())), preferred_element_type=F32)

    def fwd_vec(k, st, hb):
        fb = pl.ds(pl.multiple_of(k * SUB, SUB), SUB)
        for u in range(SUB):
            t = k * SUB + u
            row = pl.multiple_of(t * states, states)
            bb = inb[pl.ds(row, states), :]
            for g in range(groups):
                dec = jnp.exp2(nrate[g] * dk_s.at[fb, lanes(g)][u:u + 1, :])
                dec_s[pl.ds(row, states), lanes(g)] = dec
                st[g] = dec * st[g] + bb * ds_s.at[fb, lanes(g)][u:u + 1, :]
                hist[pl.ds(row + states, states), lanes(g)] = st[g]
                hb[u * states:(u + 1) * states, lanes(g)] = st[g].astype(BF16)
        return st

    def fwd_mat(k, hb):
        r32 = pl.multiple_of((k + 1) * 2 * SUB, 2 * SUB)
        r16 = pl.multiple_of((k + 1) * SUB, SUB)
        h = hb[...]
        y = jnp.dot(cmat[pl.ds(r32, 2 * SUB), :], h, preferred_element_type=F32)
        ascan[pl.ds(r16, SUB), :] = y[:SUB] + y[SUB:]
        o = nt(ab16[pl.ds(r32, 2 * SUB), :], h)
        oc_s[pl.ds(r16, SUB), :] += o[:SUB] + o[SUB:]

    def fwd(i, carry):
        st = fwd_vec(2 * i, list(carry), hb0)
        fwd_mat(2 * i - 1, hb1)
        st = fwd_vec(2 * i + 1, st, hb1)
        fwd_mat(2 * i, hb0)
        return tuple(st)
    lax.fori_loop(0, nblk // 2, fwd, st0)
    fwd_mat(nblk - 1, hb1)

    def bwd_vec(k, ca, rg, ab, al, zr):
        fb = pl.ds(pl.multiple_of(k * SUB, SUB), SUB)
        for u in reversed(range(SUB)):
            t = k * SUB + u
            row = pl.multiple_of(t * states, states)
            cc = outb[pl.ds(row, states), :]
            for g in range(groups):
                adj = cc * a_s.at[fb, lanes(g)][u:u + 1, :] + ca[g]
                hi = adj.astype(BF16)
                ab[u * states:(u + 1) * states, lanes(g)] = hi
                if lo:
                    al[u * states:(u + 1) * states, lanes(g)] = (adj - hi.astype(F32)).astype(BF16)
                ca[g] = dec_s[pl.ds(row, states), lanes(g)] * adj
                z = ca[g] * hist[pl.ds(row, states), lanes(g)]
                zr[u * states:(u + 1) * states, lanes(g)] = (z * nrate[g]).astype(BF16)
                rg[g] = rg[g] + z * d_s.at[fb, lanes(g)][u:u + 1, :]
        return ca, rg

    def bwd_mat(k, ab, al, zr):
        r32 = pl.multiple_of((k + 1) * 2 * SUB, 2 * SUB)
        r16 = pl.multiple_of((k + 1) * SUB, SUB)
        h = ab[...]
        bm = bmat[pl.ds(r32, 2 * SUB), :]
        y = jnp.dot(bm, h, preferred_element_type=F32)
        y = y[:SUB] + y[SUB:]
        if lo:
            y = y + jnp.dot(bm[:SUB], al[...], preferred_element_type=F32)
        q_s[pl.ds(r16, SUB), :] = y
        zz_s[pl.ds(r16, SUB), :] = jnp.dot(omat[...], zr[...], preferred_element_type=F32)
        o = nt(db16[pl.ds(r32, 2 * SUB), :], h)
        ic_s[pl.ds(r16, SUB), :] += o[:SUB] + o[SUB:]

    def bwd(i, carry):
        ca, rg = list(carry[0]), list(carry[1])
        k = nblk - 1 - 2 * i
        ca, rg = bwd_vec(k, ca, rg, ab0, al0, zr0)
        bwd_mat(k + 1, ab1, al1, zr1)
        ca, rg = bwd_vec(k - 1, ca, rg, ab1, al1, zr1)
        bwd_mat(k, ab0, al0, zr0)
        return tuple(ca), tuple(rg)
    z0 = tuple(jnp.zeros((states, LANES), F32) for _ in range(groups))
    _, rg = lax.fori_loop(0, nblk // 2, bwd, (tuple(a_in[:, lanes(g)] for g in range(groups)), z0))
    bwd_mat(0, ab1, al1, zr1)
    for g in range(groups):
        g_rate[:, lanes(g)] = -rg[g]

    n = tokens
    scan = ascan[SUB:SUB + n, :]
    q = q_s[SUB:SUB + n, :]
    zz = zz_s[SUB:SUB + n, :] * (1.0 / LOG2E)
    s = sig[...].astype(F32)
    g_ = gate[...].astype(F32)
    o_ = cot[...].astype(F32)
    sg = jax.nn.sigmoid(g_)
    av = a_s[...]
    k_ = skip[...]
    g_gate[...] = (o_ * (scan + k_ * s) * sg * (1.0 + g_ * (1.0 - sg))).astype(BF16)
    g_sig[...] = (d_s[...] * q + k_ * av).astype(BF16)
    rawg = (s * q + zz) * r_s[...]
    g_skip[...] = jnp.sum(s * av, 0, keepdims=True)
    g_bias[...] = jnp.sum(rawg, 0, keepdims=True)
    rr = rawg.astype(BF16)
    g_low[...] += nt(rr, w[...])
    dw[...] = lax.dot_general(low[...], rr, (((0,), (0,)), ((), ())), preferred_element_type=F32).astype(dw.dtype)

    @pl.when(step == pl.num_programs(0) - 1)
    def _():
        row = lax.broadcasted_iota(jnp.int32, (tokens, blk), 0)
        col = lax.broadcasted_iota(jnp.int32, (tokens, blk), 1)
        on = (row % SUB) == (col // states)
        pick = (lax.broadcasted_iota(jnp.int32, (blk, states), 0) % states
                == lax.broadcasted_iota(jnp.int32, (blk, states), 1)).astype(F32)
        for src, dst in ((oc_s, g_outc), (ic_s, g_inc)):
            x = jnp.where(on, src[SUB:SUB + n, :], 0.0)
            dst[...] = jnp.dot(x, pick, preferred_element_type=F32, precision=lax.Precision.HIGHEST)

WIDTH = 512

def vm(shape, dt=F32):
    return pltpu.VMEM(shape, dt)

def local_pass(low, w, bias, rate, sig, gate, cot, keep, inb, outb):
    tokens, chans = sig.shape
    n, r = rate.shape[0], low.shape[1]
    W = WIDTH
    col = lambda rows: pl.BlockSpec((rows, W), lambda j: (0, j))
    whole = lambda x: pl.BlockSpec(x.shape, lambda j: (0, 0))
    return pl.pallas_call(
        local_kernel, grid=(chans // W,),
        in_specs=[whole(low), col(r), col(1), col(n), col(tokens), col(tokens), col(tokens), whole(keep), whole(inb), whole(outb)],
        out_specs=[col(n), col(n), col(1)],
        out_shape=[jax.ShapeDtypeStruct((n, chans), F32)] * 2 + [jax.ShapeDtypeStruct((1, chans), F32)],
        scratch_shapes=[vm((tokens, W))] * 3,
        compiler_params=pltpu.CompilerParams(vmem_limit_bytes=60 << 20),
        name="local_pass",
    )(low, w, bias, rate, sig, gate, cot, keep, inb, outb)

def full_pass(low, w, bias, rate, skip, sig, gate, cot, keep, inb, outb, cmat, bmat, omat, s_in, a_in, lo=True, dwt=F32):
    tokens, chans = sig.shape
    n, r = rate.shape[0], low.shape[1]
    W = WIDTH
    blk = SUB * n
    nblk = tokens // SUB
    col = lambda rows: pl.BlockSpec((rows, W), lambda j: (0, j))
    whole = lambda x: pl.BlockSpec(x.shape, lambda j: (0, 0))
    fixed = lambda *sh: pl.BlockSpec(sh, lambda j: (0, 0))
    S = jax.ShapeDtypeStruct
    rows16, rows32 = (nblk + 2) * SUB, (nblk + 2) * 2 * SUB
    return pl.pallas_call(
        functools.partial(full_kernel, lo=lo), grid=(chans // W,),
        in_specs=[whole(low), col(r), col(1), col(n), col(1), col(tokens), col(tokens), col(tokens), whole(keep), whole(inb), whole(outb),
                  whole(cmat), whole(bmat), whole(omat), col(n), col(n)],
        out_specs=[col(tokens), col(tokens), fixed(tokens, r), fixed(tokens, n), fixed(tokens, n), col(r), col(n), col(1), col(1)],
        out_shape=[S((tokens, chans), BF16), S((tokens, chans), BF16), S((tokens, r), F32), S((tokens, n), F32), S((tokens, n), F32),
                   S((r, chans), dwt), S((n, chans), F32), S((1, chans), F32), S((1, chans), F32)],
        scratch_shapes=[vm((tokens, W))] * 5 + [vm(((tokens + 1) * n, W)), vm((tokens * n, W))] + [vm((blk, W), BF16)] * 8
            + [vm((rows16, W)), vm((rows32, W), BF16), vm((rows32, W), BF16), vm((rows16, W)), vm((rows16, W)), vm((rows16, blk)), vm((rows16, blk))],
        compiler_params=pltpu.CompilerParams(vmem_limit_bytes=60 << 20),
        name="full_pass",
    )(low, w, bias, rate, skip, sig, gate, cot, keep, inb, outb, cmat, bmat, omat, s_in, a_in)

def tables(coef_in, coef_out, keep):
    n, tokens = coef_in.shape
    nblk = tokens // SUB
    bc = lambda x: jnp.broadcast_to(x.T[:, :, None], (tokens, n, LANES)).reshape(tokens * n, LANES)
    def banded(x):
        xt = x.T
        hi = lax.reduce_precision(xt, 8, 7)
        parts = jnp.stack([hi, xt - hi])
        parts = parts.reshape(2, nblk, SUB, 1, n) * jnp.eye(SUB, dtype=F32)[None, None, :, :, None]
        m = parts.transpose(1, 0, 2, 3, 4).reshape(nblk * 2 * SUB, SUB * n)
        return jnp.pad(m, ((2 * SUB, 2 * SUB), (0, 0))).astype(BF16)
    ones = jnp.repeat(jnp.eye(SUB, dtype=F32), n, axis=1).astype(BF16)
    keepb = jnp.broadcast_to(keep[:, None], (tokens, LANES))
    return bc(coef_in), bc(coef_out), banded(coef_out), banded(coef_in), ones, keepb


def shifted(x, axis, by):
    devices = lax.axis_size(axis)
    pairs = [(i, i + by) for i in range(devices) if 0 <= i + by < devices]
    return lax.ppermute(x, axis, pairs)


def handed_on(end, total, nrate, sign):
    hops = lax.axis_size("seq")
    reach = 1
    while reach < hops:
        other, other_total = shifted((end, total), "seq", sign * reach)
        end = jnp.exp2(nrate * total) * other + end
        total = total + other_total
        reach *= 2
    return shifted(end, "seq", sign)


def shards(signal, gating, low_rank, dt_weight, dt_bias, decay_rate, skip_gain, coef_in, coef_out, segment_ids, out_grad):
    sig, gate, cot, low = signal[0], gating[0], out_grad[0], low_rank[0]
    n, owned = decay_rate.shape
    packed = jnp.concatenate([decay_rate, skip_gain[None, :], dt_bias[None, :]], 0)
    w = lax.all_gather(dt_weight, "fsdp", axis=1, tiled=True)
    params = lax.all_gather(packed, "fsdp", axis=1, tiled=True)
    rate, skip, bias = jnp.maximum(params[:-2], 1e-30), params[-2:-1], params[-1:]
    seg = segment_ids[0]
    before = shifted(seg[-1:] + 1, "seq", 1)
    prev = jnp.concatenate([before, seg[:-1] + 1])
    keep = (seg + 1 == prev).astype(F32)
    keep = keep.at[0].set(jnp.where(lax.axis_index("seq") == 0, 0.0, keep[0]))
    inb, outb, cmat, bmat, omat, keepb = tables(coef_in[0], coef_out[0], keep)
    end, back, total = local_pass(low, w, bias, rate, sig, gate, cot, keepb, inb, outb)
    nrate = rate * (-LOG2E)
    s_in = handed_on(end, total, nrate, 1)
    a_in = handed_on(back, total, nrate, -1)
    g_sig, g_gate, g_low, g_inc, g_outc, dw, g_rate, g_skip, g_bias = full_pass(
        low, w, bias, rate, skip, sig, gate, cot, keepb, inb, outb, cmat, bmat, omat, s_in, a_in, dwt=BF16)
    shares = lax.axis_size("fsdp")
    dw = lax.all_to_all(dw.reshape(-1, shares, owned), "fsdp", 1, 1)
    dw = jnp.sum(dw.astype(F32), 1)
    small = jnp.concatenate([g_rate, g_skip, g_bias], 0).reshape(n + 2, shares, owned)
    small = jnp.sum(lax.all_to_all(small, "fsdp", 1, 1), 1)
    sums = lax.psum(jnp.concatenate([dw, small], 0), "seq")
    rows = dt_weight.shape[0]
    return (g_sig[None], g_gate[None], g_low[None], g_inc.T[None], g_outc.T[None],
            sums[:rows], sums[rows:rows + n], sums[rows + n], sums[rows + n + 1])


def solution(mesh):
    return jax.shard_map(
        shards,
        mesh=mesh,
        in_specs=(
            P("fsdp", "seq", None), P("fsdp", "seq", None), P("fsdp", "seq", None),
            P(None, "fsdp"), P("fsdp"), P(None, "fsdp"), P("fsdp"),
            P("fsdp", None, "seq"), P("fsdp", None, "seq"), P("fsdp", "seq"), P("fsdp", "seq", None),
        ),
        out_specs=(
            P("fsdp", "seq", None), P("fsdp", "seq", None), P("fsdp", "seq", None),
            P("fsdp", None, "seq"), P("fsdp", None, "seq"), P(None, "fsdp"), P(None, "fsdp"), P("fsdp"), P("fsdp"),
        ),
        check_vma=False,
    )
```

```python
import functools, math
import jax, jax.numpy as jnp
from jax import lax
from jax.experimental import pallas as pl
from jax.experimental.pallas import tpu as pltpu
from jax.sharding import PartitionSpec as P

F32, BF16 = jnp.float32, jnp.bfloat16
LANES = 128
SUB = 16
LOG2E = math.log2(math.e)

PEERS = 7
PAIRS = 8
ROWS = 24
MESH = pl.DeviceIdType.MESH


def nt(x, y):
    return lax.dot_general(x, y, (((1,), (1,)), ((), ())), preferred_element_type=F32)


def wide(x, width):
    return jnp.concatenate([x] * (width // LANES), 1)


def softplus(x):
    return jnp.maximum(x, 0.0) + jnp.log1p(jnp.exp(-jnp.abs(x)))


def kernel(low, w_own, par_own, sig, gate, cot, keepb, segb, inb, outb, cmat, bmat, omat,
           g_sig, g_gate, g_low, g_inc, g_outc, g_w, g_small,
           wall, pall, lowt, keep_s, seg_in, xs, er,
           dk_s, d_s, ds_s, a_s, r_s, hist, dec_s, hb0, hb1, ab0, ab1, al0, al1, zr0, zr1,
           scan_s, a16, d16, q_s, zz_s, oc_s, ic_s,
           bsend, brecv, bsmall, brsmall, astage, asmall, drecv, srecv, acc, accs, rs, rss, fin,
           w_ss, w_rs, p_ss, p_rs, wf_ss, wf_rs, pf_ss, pf_rs, x_ss, x_rs, b_ss, b_rs, bs_ss, bs_rs,
           d_ss, d_rs, s_ss, s_rs, r_ss, r_rs, t_ss, t_rs, f_ss, f_rs, seg_ss, seg_rs, own_sem, credit):
    tokens = low.shape[0]
    width = w_own.shape[1]
    states = outb.shape[0] // tokens
    blk = SUB * states
    nblk = tokens // SUB
    seq = lax.axis_index("seq")
    me = lax.axis_index("fsdp")
    chip, core = me // 2, me % 2
    cy, cx = chip // 4, chip % 4
    sibling = (seq, chip * 2 + (1 - core))

    def target(k):
        return (seq, (((cy + k // 4) % 2) * 4 + (cx + k % 4) % 4) * 2 + core)

    def source_chip(k):
        return ((cy + k // 4) % 2) * 4 + (cx + 4 - k % 4) % 4

    def peer(i):
        return ((seq + i) % 8, me)

    def remote(src, dst, ss, rs_, dev):
        return pltpu.make_async_remote_copy(src_ref=src, dst_ref=dst, send_sem=ss, recv_sem=rs_, device_id=dev, device_id_type=MESH)

    barrier = pltpu.get_barrier_semaphore()
    for k in range(1, PAIRS):
        pl.semaphore_signal(barrier, inc=1, device_id=target(k), device_id_type=MESH)
    for i in range(1, PEERS + 1):
        pl.semaphore_signal(barrier, inc=1, device_id=peer(i), device_id_type=MESH)
    pl.semaphore_signal(barrier, inc=1, device_id=sibling, device_id_type=MESH)
    pl.semaphore_wait(barrier, PAIRS + PEERS)

    def push_w(k):
        return (remote(w_own, wall.at[2 * k], w_ss.at[k], w_rs.at[k], target(k)),
                remote(par_own, pall.at[2 * k], p_ss.at[k], p_rs.at[k], target(k)))

    def forward_w(k):
        return (remote(wall.at[2 * k], wall.at[2 * k + 1], wf_ss.at[k], wf_rs.at[k], sibling),
                remote(pall.at[2 * k], pall.at[2 * k + 1], pf_ss.at[k], pf_rs.at[k], sibling))

    def send_seg():
        return remote(segb, seg_in, seg_ss, seg_rs, peer(1))

    send_seg().start()
    for k in range(1, 4):
        for c in push_w(k):
            c.start()
    own = (pltpu.make_async_copy(w_own, wall.at[0], own_sem.at[0]), pltpu.make_async_copy(par_own, pall.at[0], own_sem.at[1]))
    for c in own:
        c.start()
    lowt[...] = low[...].T
    oc_s[...] = jnp.zeros_like(oc_s)
    ic_s[...] = jnp.zeros_like(ic_s)
    g_low[...] = jnp.zeros_like(g_low)
    for c in own:
        c.wait()
    send_seg().wait_recv()
    keep_s[...] = keepb[...]
    same = jnp.where(seg_in[SUB // 2:SUB // 2 + 1, :] == segb[0:1, :], 1.0, 0.0)
    keep_s[0:1, :] = jnp.where(seq == 0, 0.0, same)

    def columns(k, other):
        return pl.ds(pl.multiple_of((source_chip(k) * 2 + (core if other == 0 else 1 - core)) * width, width), width)

    def prepare(slot, cols):
        raw = jnp.dot(low[...], wall[slot], preferred_element_type=F32) + pall[slot, states + 1:states + 2, :]
        delta = softplus(raw)
        g = gate[:, cols].astype(F32)
        a = cot[:, cols].astype(F32) * g * jax.nn.sigmoid(g)
        dk_s[...] = jnp.where(wide(keep_s[...], width) > 0, delta, jnp.inf)
        ds = delta * sig[:, cols].astype(F32)
        ds_s[...] = ds
        a_s[...] = a
        return raw, delta, ds, a

    def rates(slot):
        return pall[slot, 0:states, :] * (-LOG2E)

    def block(i):
        return pl.ds(pl.multiple_of(i * SUB, SUB), SUB)

    def coef(ref, t):
        return wide(ref[pl.ds(pl.multiple_of(t * states, states), states), :], width)

    def local_pass(slot, cols, up, down):
        prepare(slot, cols)
        nrate = rates(slot)

        def body(i, carry):
            st, ad = carry
            for u in range(SUB):
                t = i * SUB + u
                d1 = dk_s.at[block(i), :]
                d2 = dk_s.at[block(nblk - 1 - i), :]
                v = SUB - 1 - u
                st = jnp.exp2(nrate * d1[u:u + 1, :]) * st + coef(inb, t) * ds_s.at[block(i), :][u:u + 1, :]
                ad = jnp.exp2(nrate * d2[v:v + 1, :]) * (coef(outb, tokens - 1 - t) * a_s.at[block(nblk - 1 - i), :][v:v + 1, :] + ad)
            return st, ad
        zero = jnp.zeros((states, width), F32)
        st, ad = lax.fori_loop(0, nblk, body, (zero, zero))
        total = jnp.broadcast_to(jnp.sum(dk_s[...], 0, keepdims=True), (ROWS - states, width))
        up[0:states, :] = st
        up[states:ROWS, :] = total
        down[0:states, :] = ad
        down[states:ROWS, :] = total

    def send_ends(k, i):
        return remote(xs.at[k, (seq + i) // 8], er.at[k, i - 1], x_ss.at[k, i - 1], x_rs.at[k, i - 1], peer(i))

    def first(k, carry):
        @pl.when(k > 0)
        def _():
            for c in push_w(k):
                c.wait_recv()
        for c in forward_w(k):
            c.start()

        @pl.when((k > 0) & (k < PAIRS - 3))
        def _():
            for c in push_w(k + 3):
                c.start()
        local_pass(2 * k, columns(k, 0), xs.at[k, 0, pl.ds(0, ROWS)], xs.at[k, 1, pl.ds(0, ROWS)])
        for c in forward_w(k):
            c.wait_recv()
        local_pass(2 * k + 1, columns(k, 1), xs.at[k, 0, pl.ds(ROWS, ROWS)], xs.at[k, 1, pl.ds(ROWS, ROWS)])
        for i in range(1, PEERS + 1):
            send_ends(k, i).start()
        return carry
    lax.fori_loop(0, PAIRS, first, 0)

    def entering(k, base, nrate):
        st = jnp.zeros((states, width), F32)
        ad = jnp.zeros((states, width), F32)
        for i in range(PEERS, 0, -1):
            e = er.at[k, i - 1]
            st = jnp.where(seq >= i, jnp.exp2(nrate * e[base + states:base + states + 1, :]) * st + e[base:base + states, :], st)
            e = er.at[k, PEERS - i]
            ad = jnp.where(seq + i < 8, jnp.exp2(nrate * e[base + states:base + states + 1, :]) * ad + e[base:base + states, :], ad)
        return st, ad

    def split(ref, x):
        hi = x.astype(BF16)
        rest = (x - hi.astype(F32)).astype(BF16)
        for b in range(nblk):
            ref[2 * SUB * (b + 1):2 * SUB * (b + 1) + SUB, :] = hi[b * SUB:(b + 1) * SUB]
            ref[2 * SUB * (b + 1) + SUB:2 * SUB * (b + 2), :] = rest[b * SUB:(b + 1) * SUB]

    def both(x):
        return x[:SUB] + x[SUB:]

    def full_pass(k, slot, cols, base, small):
        raw, delta, ds, a = prepare(slot, cols)
        d_s[...] = delta
        r_s[...] = jax.nn.sigmoid(raw)
        split(a16, a)
        split(d16, ds)
        nrate = rates(slot)
        st0, ad0 = entering(k, base, nrate)
        hist[0:states, :] = st0

        def fwd_vec(b, st, hb):
            for u in range(SUB):
                row = pl.multiple_of((b * SUB + u) * states, states)
                dec = jnp.exp2(nrate * dk_s.at[block(b), :][u:u + 1, :])
                dec_s[pl.ds(row, states), :] = dec
                st = dec * st + coef(inb, b * SUB + u) * ds_s.at[block(b), :][u:u + 1, :]
                hist[pl.ds(row + states, states), :] = st
                hb[u * states:(u + 1) * states, :] = st.astype(BF16)
            return st

        def rows(b, size):
            return pl.ds(pl.multiple_of((b + 1) * size, size), size)

        def fwd_mat(b, hb):
            h = hb[...]
            scan_s[rows(b, SUB), :] = both(jnp.dot(cmat[rows(b, 2 * SUB), :], h, preferred_element_type=F32))
            oc_s[rows(b, SUB), :] += both(nt(a16[rows(b, 2 * SUB), :], h))

        def fwd(i, st):
            st = fwd_vec(2 * i, st, hb0)
            fwd_mat(2 * i - 1, hb1)
            st = fwd_vec(2 * i + 1, st, hb1)
            fwd_mat(2 * i, hb0)
            return st
        lax.fori_loop(0, nblk // 2, fwd, st0)
        fwd_mat(nblk - 1, hb1)

        def bwd_vec(b, ca, rg, ab, al, zr):
            for u in reversed(range(SUB)):
                row = pl.multiple_of((b * SUB + u) * states, states)
                adj = coef(outb, b * SUB + u) * a_s.at[block(b), :][u:u + 1, :] + ca
                hi = adj.astype(BF16)
                ab[u * states:(u + 1) * states, :] = hi
                al[u * states:(u + 1) * states, :] = (adj - hi.astype(F32)).astype(BF16)
                ca = dec_s[pl.ds(row, states), :] * adj
                z = ca * hist[pl.ds(row, states), :]
                zr[u * states:(u + 1) * states, :] = (z * nrate).astype(BF16)
                rg = rg + z * d_s.at[block(b), :][u:u + 1, :]
            return ca, rg

        def bwd_mat(b, ab, al, zr):
            h = ab[...]
            bm = bmat[rows(b, 2 * SUB), :]
            q_s[rows(b, SUB), :] = (both(jnp.dot(bm, h, preferred_element_type=F32))
                                    + jnp.dot(bm[:SUB], al[...], preferred_element_type=F32))
            zz_s[rows(b, SUB), :] = jnp.dot(omat[...], zr[...], preferred_element_type=F32)
            ic_s[rows(b, SUB), :] += both(nt(d16[rows(b, 2 * SUB), :], h))

        def bwd(i, carry):
            b = nblk - 1 - 2 * i
            carry = bwd_vec(b, *carry, ab0, al0, zr0)
            bwd_mat(b + 1, ab1, al1, zr1)
            carry = bwd_vec(b - 1, *carry, ab1, al1, zr1)
            bwd_mat(b, ab0, al0, zr0)
            return carry
        _, rg = lax.fori_loop(0, nblk // 2, bwd, (ad0, jnp.zeros((states, width), F32)))
        bwd_mat(0, ab1, al1, zr1)

        q = q_s[SUB:SUB + tokens, :]
        s = sig[:, cols].astype(F32)
        g = gate[:, cols].astype(F32)
        o = cot[:, cols].astype(F32)
        sg = jax.nn.sigmoid(g)
        av = a_s[...]
        gain = pall[slot, states:states + 1, :]
        g_gate[:, cols] = (o * (scan_s[SUB:SUB + tokens, :] + gain * s) * sg * (1.0 + g * (1.0 - sg))).astype(BF16)
        g_sig[:, cols] = (d_s[...] * q + gain * av).astype(BF16)
        rawg = (s * q + zz_s[SUB:SUB + tokens, :] * (1.0 / LOG2E)) * r_s[...]
        small[0:states, :] = -rg
        small[states:ROWS, :] = jnp.zeros((ROWS - states, width), F32)
        small[states:states + 1, :] = jnp.sum(s * av, 0, keepdims=True)
        small[states + 1:states + 2, :] = jnp.sum(rawg, 0, keepdims=True)
        rr = rawg.astype(BF16)
        g_low[...] += nt(rr, wall[slot])
        return jnp.dot(lowt[...], rr, preferred_element_type=F32)

    def to_sibling(k):
        return (remote(bsend.at[k % 2], brecv.at[k % 2], b_ss.at[k], b_rs.at[k], sibling),
                remote(bsmall.at[k % 2], brsmall.at[k % 2], bs_ss.at[k], bs_rs.at[k], sibling))

    def to_owner(k):
        dev = (seq, source_chip(k) * 2 + core)
        return (remote(astage.at[k % 2], drecv.at[k - 1], d_ss.at[k], d_rs.at[k], dev),
                remote(asmall.at[k % 2], srecv.at[k - 1], s_ss.at[k], s_rs.at[k], dev))

    def second(m, carry):
        k = (m + 1) % PAIRS
        for i in range(1, PEERS + 1):
            send_ends(k, i).wait_recv()

        @pl.when(m >= 2)
        def _():
            for c in to_sibling(m - 1):
                c.wait_send()
            pl.semaphore_wait(credit, 1)
        bsend[k % 2] = full_pass(k, 2 * k + 1, columns(k, 1), ROWS, bsmall.at[k % 2])
        for c in to_sibling(k):
            c.start()

        @pl.when((m >= 2) & (m < PAIRS - 1))
        def _():
            for c in to_owner(m - 1):
                c.wait_send()
        acc[...] = full_pass(k, 2 * k, columns(k, 0), 0, accs)
        for c in to_sibling(k):
            c.wait_recv()
        acc[...] += brecv[k % 2]
        accs[...] += brsmall[k % 2]

        @pl.when(m < PAIRS - 2)
        def _():
            pl.semaphore_signal(credit, inc=1, device_id=sibling, device_id_type=MESH)

        @pl.when(m < PAIRS - 1)
        def _():
            astage[k % 2] = acc[...].astype(BF16)
            asmall[k % 2] = accs[...]
            for c in to_owner(k):
                c.start()
        return carry
    lax.fori_loop(0, PAIRS, second, 0)

    def add_in(k, carry):
        for c in to_owner(k):
            c.wait_recv()
        acc[...] += drecv[k - 1].astype(F32)
        accs[...] += srecv[k - 1]
        return carry
    lax.fori_loop(1, PAIRS, add_in, 0)

    rank = acc.shape[0]
    part = rank // 8

    def part_of(i):
        return pl.ds(pl.multiple_of(((seq + i) % 8) * part, part), part)

    def scatter(i):
        return (remote(acc.at[part_of(i)], rs.at[seq], r_ss.at[i - 1], r_rs.at[i - 1], peer(i)),
                remote(accs, rss.at[seq], t_ss.at[i - 1], t_rs.at[i - 1], peer(i)))

    def arrived(i):
        j = (seq + 8 - i) % 8
        return (remote(acc.at[part_of(0)], rs.at[j], r_ss.at[i - 1], r_rs.at[i - 1], peer(i)),
                remote(accs, rss.at[j], t_ss.at[i - 1], t_rs.at[i - 1], peer(i)))

    def gather(i):
        return remote(fin.at[part_of(0)], fin.at[part_of(0)], f_ss.at[i - 1], f_rs.at[i - 1], peer(i))

    def gathered(i):
        return remote(fin.at[part_of(8 - i)], fin.at[part_of(8 - i)], f_ss.at[i - 1], f_rs.at[i - 1], peer(i))

    for i in range(1, PEERS + 1):
        for c in scatter(i):
            c.start()
    rs[seq] = acc[part_of(0), :]
    rss[seq] = accs[...]
    for i in range(1, PEERS + 1):
        for c in arrived(i):
            c.wait_recv()
    total, small = rs[0], rss[0]
    for i in range(1, PEERS + 1):
        total = total + rs[i]
        small = small + rss[i]
    fin[part_of(0), :] = total
    g_small[...] = small
    for i in range(1, PEERS + 1):
        gather(i).start()

    row = lax.broadcasted_iota(jnp.int32, (tokens, blk), 0)
    col = lax.broadcasted_iota(jnp.int32, (tokens, blk), 1)
    on = (row % SUB) == (col // states)
    pick = jnp.where(lax.broadcasted_iota(jnp.int32, (blk, states), 0) % states
                     == lax.broadcasted_iota(jnp.int32, (blk, states), 1), 1.0, 0.0)
    for src, dst in ((oc_s, g_outc), (ic_s, g_inc)):
        x = jnp.where(on, src[SUB:SUB + tokens, :], 0.0)
        dst[...] = jnp.dot(x, pick, preferred_element_type=F32, precision=lax.Precision.HIGHEST)

    for i in range(1, PEERS + 1):
        gathered(i).wait_recv()
    g_w[...] = fin[...]

    send_seg().wait_send()
    for k in range(PAIRS):
        for c in forward_w(k):
            c.wait_send()
        for i in range(1, PEERS + 1):
            send_ends(k, i).wait_send()
    for k in range(1, PAIRS):
        for c in push_w(k):
            c.wait_send()
    for k in (PAIRS - 1, 0):
        for c in to_sibling(k):
            c.wait_send()
    for k in (PAIRS - 2, PAIRS - 1):
        for c in to_owner(k):
            c.wait_send()
    for i in range(1, PEERS + 1):
        for c in scatter(i):
            c.wait_send()
        gather(i).wait_send()


def run(low, w, par, sig, gate, cot, keepb, segb, inb, outb, cmat, bmat, omat):
    tokens, chans = sig.shape
    rank, width = w.shape
    n = outb.shape[0] // tokens
    blk = SUB * n
    nblk = tokens // SUB
    rows16, rows32 = (nblk + 2) * SUB, (nblk + 2) * 2 * SUB
    S = jax.ShapeDtypeStruct
    vm = lambda *shape: pltpu.VMEM(shape, F32)
    vb = lambda *shape: pltpu.VMEM(shape, BF16)
    dma = lambda *shape: pltpu.SemaphoreType.DMA(shape)
    scratch = [
        vb(16, rank, width), vm(16, ROWS, width), vb(rank, tokens), vm(tokens, LANES), vm(SUB, LANES),
        vm(PAIRS, 2, 2 * ROWS, width), vm(PAIRS, PEERS, 2 * ROWS, width),
    ] + [vm(tokens, width)] * 5 + [vm((tokens + 1) * n, width), vm(tokens * n, width)] + [vb(blk, width)] * 8 + [
        vm(rows16, width), vb(rows32, width), vb(rows32, width), vm(rows16, width), vm(rows16, width), vm(rows16, blk), vm(rows16, blk),
        vm(2, rank, width), vm(2, rank, width), vm(2, ROWS, width), vm(2, ROWS, width),
        vb(2, rank, width), vm(2, ROWS, width), vb(PAIRS - 1, rank, width), vm(PAIRS - 1, ROWS, width),
        vm(rank, width), vm(ROWS, width), vm(8, rank // 8, width), vm(8, ROWS, width), vm(rank, width),
    ] + [dma(PAIRS)] * 8 + [dma(PAIRS, PEERS)] * 2 + [dma(PAIRS)] * 8 + [dma(PEERS)] * 6 + [
        pltpu.SemaphoreType.DMA, pltpu.SemaphoreType.DMA, dma(2), pltpu.SemaphoreType.REGULAR]
    points = tokens * n * chans
    return pl.pallas_call(
        kernel,
        in_specs=[pl.BlockSpec(memory_space=pltpu.VMEM)] * 13,
        out_specs=[pl.BlockSpec(memory_space=pltpu.VMEM)] * 7,
        out_shape=[S((tokens, chans), BF16), S((tokens, chans), BF16), S((tokens, rank), F32), S((tokens, n), F32),
                   S((tokens, n), F32), S((rank, width), F32), S((ROWS, width), F32)],
        scratch_shapes=scratch,
        cost_estimate=pl.CostEstimate(flops=30 * points, bytes_accessed=20 << 20, transcendentals=3 * points),
        compiler_params=pltpu.CompilerParams(vmem_limit_bytes=63 << 20, collective_id=0, has_side_effects=True),
        name="scan_backward",
    )(low, w, par, sig, gate, cot, keepb, segb, inb, outb, cmat, bmat, omat)


def tables(coef_in, coef_out):
    n, tokens = coef_in.shape
    nblk = tokens // SUB
    bc = lambda x: jnp.broadcast_to(x.T[:, :, None], (tokens, n, LANES)).reshape(tokens * n, LANES)

    def banded(x):
        xt = x.T
        hi = lax.reduce_precision(xt, 8, 7)
        parts = jnp.stack([hi, xt - hi]).reshape(2, nblk, SUB, 1, n) * jnp.eye(SUB, dtype=F32)[None, None, :, :, None]
        m = parts.transpose(1, 0, 2, 3, 4).reshape(nblk * 2 * SUB, SUB * n)
        return jnp.pad(m, ((2 * SUB, 2 * SUB), (0, 0))).astype(BF16)
    ones = jnp.repeat(jnp.eye(SUB, dtype=F32), n, axis=1).astype(BF16)
    return bc(coef_in), bc(coef_out), banded(coef_out), banded(coef_in), ones


def shards(signal, gating, low_rank, dt_weight, dt_bias, decay_rate, skip_gain, coef_in, coef_out, segment_ids, out_grad):
    n, owned = decay_rate.shape
    par = jnp.concatenate([jnp.maximum(decay_rate, 1e-30), skip_gain[None, :], dt_bias[None, :],
                           jnp.zeros((ROWS - n - 2, owned), F32)], 0)
    seg = segment_ids[0].astype(F32)
    keep = jnp.concatenate([jnp.zeros((1,), F32), (seg[1:] == seg[:-1]).astype(F32)])
    keepb = jnp.broadcast_to(keep[:, None], (keep.shape[0], LANES))
    segb = jnp.broadcast_to(jnp.repeat(jnp.stack([seg[0], seg[-1]]), SUB // 2)[:, None], (SUB, LANES))
    g_sig, g_gate, g_low, g_inc, g_outc, g_w, g_small = run(
        low_rank[0], dt_weight, par, signal[0], gating[0], out_grad[0], keepb, segb, *tables(coef_in[0], coef_out[0]))
    return (g_sig[None], g_gate[None], g_low[None], g_inc.T[None], g_outc.T[None],
            g_w, g_small[:n], g_small[n], g_small[n + 1])


def solution(mesh):
    return jax.shard_map(
        shards,
        mesh=mesh,
        in_specs=(
            P("fsdp", "seq", None), P("fsdp", "seq", None), P("fsdp", "seq", None),
            P(None, "fsdp"), P("fsdp"), P(None, "fsdp"), P("fsdp"),
            P("fsdp", None, "seq"), P("fsdp", None, "seq"), P("fsdp", "seq"), P("fsdp", "seq", None),
        ),
        out_specs=(
            P("fsdp", "seq", None), P("fsdp", "seq", None), P("fsdp", "seq", None),
            P("fsdp", None, "seq"), P("fsdp", None, "seq"), P(None, "fsdp"), P(None, "fsdp"), P("fsdp"), P("fsdp"),
        ),
        check_vma=False,
    )
```

```python
import functools, math
import jax, jax.numpy as jnp
from jax import lax
from jax.experimental import pallas as pl
from jax.experimental.pallas import tpu as pltpu
from jax.sharding import PartitionSpec as P

F32, BF16 = jnp.float32, jnp.bfloat16
LANES = 128
SUB = 16
LOG2E = math.log2(math.e)

PEERS = 7
PAIRS = 8
ROWS = 24
MESH = pl.DeviceIdType.MESH


def nt(x, y):
    return lax.dot_general(x, y, (((1,), (1,)), ((), ())), preferred_element_type=F32)


def wide(x, width):
    return jnp.concatenate([x] * (width // LANES), 1)


def softplus(x):
    return jnp.maximum(x, 0.0) + jnp.log1p(jnp.exp(-jnp.abs(x)))


def kernel(low, w_own, rate_own, skip_own, bias_own, sig_hbm, gate_hbm, cot_hbm, seg, c_in, c_out,
           g_sig, g_gate, g_low, g_inc, g_outc, g_w, g_rate, g_skip, g_bias,
           sig, gate, cot, par_own, wall, pall, lowt, seg_s, keep_s, inb, outb, ones, xs, er,
           dk_s, d_s, ds_s, a_s, r_s, hist, dec_s, y0, y1, q0, q1, z0, z1,
           scan_s, q_s, zz_s, oc_s, ic_s,
           bsend, brecv, bsmall, brsmall, astage, asmall, drecv, srecv, acc, accs, rs, rss, fin,
           w_ss, w_rs, p_ss, p_rs, wf_ss, wf_rs, pf_ss, pf_rs, x_ss, x_rs, b_ss, b_rs, bs_ss, bs_rs,
           d_ss, d_rs, s_ss, s_rs, r_ss, r_rs, t_ss, t_rs, f_ss, f_rs, h_ss, h_rs, seg_ss, seg_rs, own_sem, credit):
    tokens = low.shape[0]
    width = w_own.shape[1]
    states = rate_own.shape[0]
    half = states // 2
    blk = SUB * half
    nblk = tokens // SUB
    seq = lax.axis_index("seq")
    me = lax.axis_index("fsdp")
    chip, core = me // 2, me % 2
    cy, cx = chip // 4, chip % 4
    sibling = (seq, chip * 2 + (1 - core))

    def offset(k):
        late = k // 6
        r = k % 3
        return (1 - late) * (k // 3) + late * (k % 2), (1 - late) * (r + r // 2) + 2 * late

    def device(dy, dx):
        return (seq, (((cy + dy) % 2) * 4 + (cx + dx) % 4) * 2 + core)

    def target(k):
        return device(*offset(k))

    def source_chip(k):
        dy, dx = offset(k)
        return ((cy + dy) % 2) * 4 + (cx + 4 - dx) % 4

    def peer(i):
        return ((seq + i) % 8, me)

    def remote(src, dst, ss, rs_, dev):
        return pltpu.make_async_remote_copy(src_ref=src, dst_ref=dst, send_sem=ss, recv_sem=rs_, device_id=dev, device_id_type=MESH)

    barrier = pltpu.get_barrier_semaphore()
    for k in range(1, PAIRS):
        pl.semaphore_signal(barrier, inc=1, device_id=target(k), device_id_type=MESH)
    for i in range(1, PEERS + 1):
        pl.semaphore_signal(barrier, inc=1, device_id=peer(i), device_id_type=MESH)
    pl.semaphore_signal(barrier, inc=1, device_id=sibling, device_id_type=MESH)
    pl.semaphore_wait(barrier, PAIRS + PEERS)

    def push_p(k):
        return remote(par_own, pall.at[2 * k], p_ss.at[k], p_rs.at[k], target(k))

    def hop(src, k, dev, part=None):
        if part is None:
            return remote(src, wall.at[2 * k], w_ss.at[k], w_rs.at[k], dev)
        rows = pl.ds(part * (w_own.shape[0] // 2), w_own.shape[0] // 2)
        return remote(src.at[rows], wall.at[2 * k, rows], h_ss.at[k - 6, part], h_rs.at[k - 6, part], dev)

    right, left, across = device(0, 1), device(0, 3), device(1, 0)

    def hops(k):
        if k == 1:
            return [hop(w_own, 1, right)]
        if k == 2:
            return [hop(w_own, 2, left)]
        if k == 3:
            return [hop(w_own, 3, across)]
        if k == 4:
            return [hop(wall.at[6], 4, right)]
        if k == 5:
            return [hop(wall.at[6], 5, left)]
        if k == 6:
            return [hop(wall.at[2], 6, right, 0), hop(wall.at[4], 6, left, 1)]
        return [hop(wall.at[12], 7, across, 0), hop(wall.at[12], 7, across, 1)]

    def forward_w(k):
        return (remote(wall.at[2 * k], wall.at[2 * k + 1], wf_ss.at[k], wf_rs.at[k], sibling),
                remote(pall.at[2 * k], pall.at[2 * k + 1], pf_ss.at[k], pf_rs.at[k], sibling))

    def send_seg():
        return remote(seg_s.at[pl.ds(tokens, 8)], seg_s.at[pl.ds(0, 8)], seg_ss, seg_rs, peer(1))

    inputs = [pltpu.make_async_copy(a, b, own_sem.at[2 + i]) for i, (a, b) in enumerate(((sig_hbm, sig), (gate_hbm, gate), (cot_hbm, cot)))]
    for k in (1, 2, 3):
        for c in hops(k):
            c.start()
    own = pltpu.make_async_copy(w_own, wall.at[0], own_sem.at[0])
    own.start()
    for c in inputs:
        c.start()
    par_own[0:states, :] = jnp.maximum(rate_own[...], 1e-30)
    par_own[states:ROWS, :] = jnp.zeros((ROWS - states, width), F32)
    par_own[states:states + 1, :] = skip_own[...]
    par_own[states + 1:states + 2, :] = bias_own[...]
    for k in range(1, PAIRS):
        push_p(k).start()
    ownp = pltpu.make_async_copy(par_own, pall.at[0], own_sem.at[1])
    ownp.start()
    seg_s[8:8 + tokens, :] = jnp.broadcast_to(seg[...].astype(F32), (LANES, tokens)).T
    send_seg().start()
    own.wait()
    ownp.wait()
    for c in forward_w(0):
        c.start()
    for t in range(tokens):
        inb[t * states:(t + 1) * states, :] = jnp.broadcast_to(c_in[:, t:t + 1], (states, LANES))
        outb[t * states:(t + 1) * states, :] = jnp.broadcast_to(c_out[:, t:t + 1], (states, LANES))
    ones[...] = jnp.where(lax.broadcasted_iota(jnp.int32, (SUB, 2 * blk), 1) % blk // half
                          == lax.broadcasted_iota(jnp.int32, (SUB, 2 * blk), 0), 1.0, 0.0).astype(BF16)
    lowt[...] = low[...].T
    oc_s[...] = jnp.zeros_like(oc_s)
    ic_s[...] = jnp.zeros_like(ic_s)
    g_low[...] = jnp.zeros_like(g_low)
    send_seg().wait_recv()
    keep_s[...] = jnp.where(seg_s[8:8 + tokens, :] == seg_s[7:7 + tokens, :], 1.0, 0.0)
    keep_s[0:1, :] = jnp.where(seq == 0, 0.0, keep_s[0:1, :])
    for c in inputs:
        c.wait()

    def columns(k, other):
        return pl.ds(pl.multiple_of((source_chip(k) * 2 + (core if other == 0 else 1 - core)) * width, width), width)

    def prepare(slot, cols):
        raw = jnp.dot(low[...], wall[slot], preferred_element_type=F32) + pall[slot, states + 1:states + 2, :]
        delta = softplus(raw)
        g = gate[:, cols].astype(F32)
        a = cot[:, cols].astype(F32) * g * jax.nn.sigmoid(g)
        dk_s[...] = jnp.where(wide(keep_s[...], width) > 0, delta, jnp.inf)
        ds = delta * sig[:, cols].astype(F32)
        ds_s[...] = ds
        a_s[...] = a
        return raw, delta, ds, a

    def rates(slot):
        return pall[slot, 0:states, :] * (-LOG2E)

    def block(i):
        return pl.ds(pl.multiple_of(i * SUB, SUB), SUB)

    def coef(ref, t):
        return wide(ref[pl.ds(pl.multiple_of(t * states, states), states), :], width)

    def local_pass(slot, cols, up, down):
        prepare(slot, cols)
        nrate = rates(slot)

        def body(i, carry):
            st, ad = carry
            for u in range(SUB):
                t = i * SUB + u
                d1 = dk_s.at[block(i), :]
                d2 = dk_s.at[block(nblk - 1 - i), :]
                v = SUB - 1 - u
                st = jnp.exp2(nrate * d1[u:u + 1, :]) * st + coef(inb, t) * ds_s.at[block(i), :][u:u + 1, :]
                ad = jnp.exp2(nrate * d2[v:v + 1, :]) * (coef(outb, tokens - 1 - t) * a_s.at[block(nblk - 1 - i), :][v:v + 1, :] + ad)
            return st, ad
        zero = jnp.zeros((states, width), F32)
        st, ad = lax.fori_loop(0, nblk, body, (zero, zero))
        total = jnp.broadcast_to(jnp.sum(dk_s[...], 0, keepdims=True), (ROWS - states, width))
        up[0:states, :] = st
        up[states:ROWS, :] = total
        down[0:states, :] = ad
        down[states:ROWS, :] = total

    def send_ends(k, i):
        return remote(xs.at[k, (seq + i) // 8], er.at[k, i - 1], x_ss.at[k, i - 1], x_rs.at[k, i - 1], peer(i))

    def shared(k):
        for c in forward_w(k):
            c.start()

    def came(k):
        for c in hops(k):
            c.wait_recv()
        push_p(k).wait_recv()

    def first(k, carry):
        @pl.when(k == 1)
        def _():
            for j in (1, 2, 3):
                came(j)
            for j in (4, 5, 6):
                for c in hops(j):
                    c.start()
            for j in (1, 2, 3):
                shared(j)

        @pl.when(k == 4)
        def _():
            for j in (4, 5):
                came(j)
                shared(j)

        @pl.when(k == 5)
        def _():
            came(6)
            for c in hops(7):
                c.start()
            shared(6)

        @pl.when(k == 7)
        def _():
            came(7)
            shared(7)
        local_pass(2 * k, columns(k, 0), xs.at[k, 0, pl.ds(0, ROWS)], xs.at[k, 1, pl.ds(0, ROWS)])
        for c in forward_w(k):
            c.wait_recv()
        local_pass(2 * k + 1, columns(k, 1), xs.at[k, 0, pl.ds(ROWS, ROWS)], xs.at[k, 1, pl.ds(ROWS, ROWS)])
        for i in range(1, PEERS + 1):
            send_ends(k, i).start()
        return carry
    lax.fori_loop(0, PAIRS, first, 0)

    def entering(k, base, nrate):
        st = jnp.zeros((states, width), F32)
        ad = jnp.zeros((states, width), F32)
        for i in range(PEERS, 0, -1):
            e = er.at[k, i - 1]
            st = jnp.where(seq >= i, jnp.exp2(nrate * e[base + states:base + states + 1, :]) * st + e[base:base + states, :], st)
            e = er.at[k, PEERS - i]
            ad = jnp.where(seq + i < 8, jnp.exp2(nrate * e[base + states:base + states + 1, :]) * ad + e[base:base + states, :], ad)
        return st, ad

    def folded(x):
        return x[:half] + x[half:]

    def lane_groups(x):
        return functools.reduce(lambda p, q: p + q, [x[:, g * LANES:(g + 1) * LANES] for g in range(width // LANES)])

    def ones_dot(x):
        return jnp.dot(ones[:, 0:x.shape[0]], x, preferred_element_type=F32)

    def full_pass(k, slot, cols, base, small):
        raw, delta, ds, a = prepare(slot, cols)
        d_s[...] = delta
        r_s[...] = jax.nn.sigmoid(raw)
        nrate = rates(slot)
        st0, ad0 = entering(k, base, nrate)
        hist[0:states, :] = st0

        def fwd_vec(b, st, y):
            held = None
            for u in range(SUB):
                row = pl.multiple_of((b * SUB + u) * states, states)
                here = pl.ds(row, states)
                dec = jnp.exp2(nrate * dk_s.at[block(b), :][u:u + 1, :])
                dec_s[here, :] = dec
                st = dec * st + coef(inb, b * SUB + u) * ds_s.at[block(b), :][u:u + 1, :]
                hist[pl.ds(row + states, states), :] = st
                oc_s[here, :] += lane_groups(st * a_s.at[block(b), :][u:u + 1, :])
                part = folded(st * coef(outb, b * SUB + u))
                if u % 2:
                    y[(u - 1) * half:(u + 1) * half, :] = jnp.concatenate([held, part], 0).astype(BF16)
                held = part
            return st

        def rows(b):
            return pl.ds(pl.multiple_of((b + 1) * SUB, SUB), SUB)

        def fwd_mat(b, y):
            scan_s[rows(b), :] = ones_dot(y[...])

        def fwd(i, st):
            st = fwd_vec(2 * i, st, y0)
            fwd_mat(2 * i - 1, y1)
            st = fwd_vec(2 * i + 1, st, y1)
            fwd_mat(2 * i, y0)
            return st
        lax.fori_loop(0, nblk // 2, fwd, st0)
        fwd_mat(nblk - 1, y1)

        def bwd_vec(b, ca, rg, qb, zb):
            held = None
            for u in reversed(range(SUB)):
                row = pl.multiple_of((b * SUB + u) * states, states)
                here = pl.ds(row, states)
                adj = coef(outb, b * SUB + u) * a_s.at[block(b), :][u:u + 1, :] + ca
                ic_s[here, :] += lane_groups(adj * ds_s.at[block(b), :][u:u + 1, :])
                ca = dec_s[here, :] * adj
                z = ca * hist[here, :]
                rg = rg + z * d_s.at[block(b), :][u:u + 1, :]
                part = folded(adj * coef(inb, b * SUB + u)), folded(z * nrate)
                if u % 2 == 0:
                    at = slice(u * half, (u + 2) * half)
                    pair = jnp.concatenate([part[0], held[0]], 0)
                    hi = pair.astype(BF16)
                    qb[at, :] = hi
                    qb[blk + u * half:blk + (u + 2) * half, :] = (pair - hi.astype(F32)).astype(BF16)
                    zb[at, :] = jnp.concatenate([part[1], held[1]], 0).astype(BF16)
                held = part
            return ca, rg

        def bwd_mat(b, qb, zb):
            q_s[rows(b), :] = ones_dot(qb[...])
            zz_s[rows(b), :] = ones_dot(zb[...])

        def bwd(i, carry):
            b = nblk - 1 - 2 * i
            carry = bwd_vec(b, *carry, q0, z0)
            bwd_mat(b + 1, q1, z1)
            carry = bwd_vec(b - 1, *carry, q1, z1)
            bwd_mat(b, q0, z0)
            return carry
        _, rg = lax.fori_loop(0, nblk // 2, bwd, (ad0, jnp.zeros((states, width), F32)))
        bwd_mat(0, q1, z1)

        q = q_s[SUB:SUB + tokens, :]
        s = sig[:, cols].astype(F32)
        g = gate[:, cols].astype(F32)
        o = cot[:, cols].astype(F32)
        sg = jax.nn.sigmoid(g)
        av = a_s[...]
        gain = pall[slot, states:states + 1, :]
        g_gate[:, cols] = (o * (scan_s[SUB:SUB + tokens, :] + gain * s) * sg * (1.0 + g * (1.0 - sg))).astype(BF16)
        g_sig[:, cols] = (d_s[...] * q + gain * av).astype(BF16)
        rawg = (s * q + zz_s[SUB:SUB + tokens, :] * (1.0 / LOG2E)) * r_s[...]
        small[0:states, :] = -rg
        small[states:ROWS, :] = jnp.zeros((ROWS - states, width), F32)
        small[states:states + 1, :] = jnp.sum(s * av, 0, keepdims=True)
        small[states + 1:states + 2, :] = jnp.sum(rawg, 0, keepdims=True)
        rr = rawg.astype(BF16)
        g_low[...] += nt(rr, wall[slot])
        return jnp.dot(lowt[...], rr, preferred_element_type=F32)

    def to_sibling(k):
        return (remote(bsend.at[k % 2], brecv.at[k % 2], b_ss.at[k], b_rs.at[k], sibling),
                remote(bsmall.at[k % 2], brsmall.at[k % 2], bs_ss.at[k], bs_rs.at[k], sibling))

    def to_owner(k):
        dev = (seq, source_chip(k) * 2 + core)
        return (remote(astage.at[k % 2], drecv.at[k - 1], d_ss.at[k], d_rs.at[k], dev),
                remote(asmall.at[k % 2], srecv.at[k - 1], s_ss.at[k], s_rs.at[k], dev))

    def second(m, carry):
        k = (m + 1) % PAIRS
        for i in range(1, PEERS + 1):
            send_ends(k, i).wait_recv()

        @pl.when(m >= 2)
        def _():
            for c in to_sibling(m - 1):
                c.wait_send()
            pl.semaphore_wait(credit, 1)
        bsend[k % 2] = full_pass(k, 2 * k + 1, columns(k, 1), ROWS, bsmall.at[k % 2])
        for c in to_sibling(k):
            c.start()

        @pl.when((m >= 2) & (m < PAIRS - 1))
        def _():
            for c in to_owner(m - 1):
                c.wait_send()
        acc[...] = full_pass(k, 2 * k, columns(k, 0), 0, accs)
        for c in to_sibling(k):
            c.wait_recv()
        acc[...] += brecv[k % 2]
        accs[...] += brsmall[k % 2]

        @pl.when(m < PAIRS - 2)
        def _():
            pl.semaphore_signal(credit, inc=1, device_id=sibling, device_id_type=MESH)

        @pl.when(m < PAIRS - 1)
        def _():
            astage[k % 2] = acc[...].astype(BF16)
            asmall[k % 2] = accs[...]
            for c in to_owner(k):
                c.start()
        return carry
    lax.fori_loop(0, PAIRS, second, 0)

    def add_in(k, carry):
        for c in to_owner(k):
            c.wait_recv()
        acc[...] += drecv[k - 1].astype(F32)
        accs[...] += srecv[k - 1]
        return carry
    lax.fori_loop(1, PAIRS, add_in, 0)

    rank = acc.shape[0]
    part = rank // 8

    def part_of(i):
        return pl.ds(pl.multiple_of(((seq + i) % 8) * part, part), part)

    def scatter(i):
        return (remote(acc.at[part_of(i)], rs.at[seq], r_ss.at[i - 1], r_rs.at[i - 1], peer(i)),
                remote(accs, rss.at[seq], t_ss.at[i - 1], t_rs.at[i - 1], peer(i)))

    def arrived(i):
        j = (seq + 8 - i) % 8
        return (remote(acc.at[part_of(0)], rs.at[j], r_ss.at[i - 1], r_rs.at[i - 1], peer(i)),
                remote(accs, rss.at[j], t_ss.at[i - 1], t_rs.at[i - 1], peer(i)))

    def gather(i):
        return remote(fin.at[part_of(0)], fin.at[part_of(0)], f_ss.at[i - 1], f_rs.at[i - 1], peer(i))

    def gathered(i):
        return remote(fin.at[part_of(8 - i)], fin.at[part_of(8 - i)], f_ss.at[i - 1], f_rs.at[i - 1], peer(i))

    for i in range(1, PEERS + 1):
        for c in scatter(i):
            c.start()
    rs[seq] = acc[part_of(0), :]
    rss[seq] = accs[...]
    for i in range(1, PEERS + 1):
        for c in arrived(i):
            c.wait_recv()
    total, small = rs[0], rss[0]
    for i in range(1, PEERS + 1):
        total = total + rs[i]
        small = small + rss[i]
    fin[part_of(0), :] = total
    g_rate[...] = small[0:states]
    g_skip[...] = small[states:states + 1]
    g_bias[...] = small[states + 1:states + 2]
    for i in range(1, PEERS + 1):
        gather(i).start()

    for src, dst in ((oc_s, g_outc), (ic_s, g_inc)):
        for n in range(states):
            dst[n:n + 1, :] = jnp.sum(src[pl.ds(n, tokens, stride=states), :].T, 0, keepdims=True)

    for i in range(1, PEERS + 1):
        gathered(i).wait_recv()
    g_w[...] = fin[...]

    send_seg().wait_send()
    for k in range(PAIRS):
        for c in forward_w(k):
            c.wait_send()
        for i in range(1, PEERS + 1):
            send_ends(k, i).wait_send()
    for k in range(1, PAIRS):
        for c in hops(k):
            c.wait_send()
        push_p(k).wait_send()
    for k in (PAIRS - 1, 0):
        for c in to_sibling(k):
            c.wait_send()
    for k in (PAIRS - 2, PAIRS - 1):
        for c in to_owner(k):
            c.wait_send()
    for i in range(1, PEERS + 1):
        for c in scatter(i):
            c.wait_send()
        gather(i).wait_send()


def run(low, w, rate, skip, bias, sig, gate, cot, seg, c_in, c_out):
    tokens, chans = sig.shape
    rank, width = w.shape
    n = rate.shape[0]
    blk = SUB * n // 2
    rows16 = (tokens // SUB + 2) * SUB
    S = jax.ShapeDtypeStruct
    vm = lambda *shape: pltpu.VMEM(shape, F32)
    vb = lambda *shape: pltpu.VMEM(shape, BF16)
    dma = lambda *shape: pltpu.SemaphoreType.DMA(shape)
    scratch = [vb(tokens, chans)] * 3 + [
        vm(ROWS, width), vb(16, rank, width), vm(16, ROWS, width), vb(rank, tokens), vm(tokens + 8, LANES), vm(tokens, LANES),
        vm(tokens * n, LANES), vm(tokens * n, LANES), vb(SUB, 2 * blk),
        vm(PAIRS, 2, 2 * ROWS, width), vm(PAIRS, PEERS, 2 * ROWS, width),
    ] + [vm(tokens, width)] * 5 + [vm((tokens + 1) * n, width), vm(tokens * n, width)] + [
        vb(blk, width), vb(blk, width), vb(2 * blk, width), vb(2 * blk, width), vb(blk, width), vb(blk, width),
        vm(rows16, width), vm(rows16, width), vm(rows16, width), vm(tokens * n, LANES), vm(tokens * n, LANES),
        vm(2, rank, width), vm(2, rank, width), vm(2, ROWS, width), vm(2, ROWS, width),
        vb(2, rank, width), vm(2, ROWS, width), vb(PAIRS - 1, rank, width), vm(PAIRS - 1, ROWS, width),
        vm(rank, width), vm(ROWS, width), vm(8, rank // 8, width), vm(8, ROWS, width), vm(rank, width),
    ] + [dma(PAIRS)] * 8 + [dma(PAIRS, PEERS)] * 2 + [dma(PAIRS)] * 8 + [dma(PEERS)] * 6 + [dma(2, 2)] * 2 + [
        pltpu.SemaphoreType.DMA, pltpu.SemaphoreType.DMA, dma(5), pltpu.SemaphoreType.REGULAR]
    points = tokens * n * chans
    vmem, hbm = pl.BlockSpec(memory_space=pltpu.VMEM), pl.BlockSpec(memory_space=pl.ANY)
    return pl.pallas_call(
        kernel,
        in_specs=[vmem] * 5 + [hbm] * 3 + [vmem] * 3,
        out_specs=[vmem] * 9,
        out_shape=[S((tokens, chans), BF16), S((tokens, chans), BF16), S((tokens, rank), F32), S((n, tokens), F32),
                   S((n, tokens), F32), S((rank, width), F32), S((n, width), F32), S((1, width), F32), S((1, width), F32)],
        scratch_shapes=scratch,
        cost_estimate=pl.CostEstimate(flops=30 * points, bytes_accessed=20 << 20, transcendentals=3 * points),
        compiler_params=pltpu.CompilerParams(vmem_limit_bytes=63 << 20, collective_id=0, has_side_effects=True),
        name="scan_backward",
    )(low, w, rate, skip, bias, sig, gate, cot, seg, c_in, c_out)


def shards(signal, gating, low_rank, dt_weight, dt_bias, decay_rate, skip_gain, coef_in, coef_out, segment_ids, out_grad):
    g_sig, g_gate, g_low, g_inc, g_outc, g_w, g_rate, g_skip, g_bias = run(
        low_rank[0], dt_weight, decay_rate, skip_gain[None], dt_bias[None], signal[0], gating[0], out_grad[0],
        segment_ids, coef_in[0], coef_out[0])
    return (g_sig[None], g_gate[None], g_low[None], g_inc[None], g_outc[None], g_w, g_rate, g_skip[0], g_bias[0])


def solution(mesh):
    return jax.shard_map(
        shards,
        mesh=mesh,
        in_specs=(
            P("fsdp", "seq", None), P("fsdp", "seq", None), P("fsdp", "seq", None),
            P(None, "fsdp"), P("fsdp"), P(None, "fsdp"), P("fsdp"),
            P("fsdp", None, "seq"), P("fsdp", None, "seq"), P("fsdp", "seq"), P("fsdp", "seq", None),
        ),
        out_specs=(
            P("fsdp", "seq", None), P("fsdp", "seq", None), P("fsdp", "seq", None),
            P("fsdp", None, "seq"), P("fsdp", None, "seq"), P(None, "fsdp"), P(None, "fsdp"), P("fsdp"), P("fsdp"),
        ),
        check_vma=False,
    )
```

```python
import functools, math
import jax, jax.numpy as jnp
from jax import lax
from jax.experimental import pallas as pl
from jax.experimental.pallas import tpu as pltpu
from jax.sharding import PartitionSpec as P

F32, BF16 = jnp.float32, jnp.bfloat16
LANES = 128
SUB = 16
LOG2E = math.log2(math.e)

PEERS = 7
PAIRS = 8
ROWS = 24
ENDS = 40
MESH = pl.DeviceIdType.MESH


def nt(x, y):
    return lax.dot_general(x, y, (((1,), (1,)), ((), ())), preferred_element_type=F32)


def wide(x, width):
    return jnp.concatenate([x] * (width // LANES), 1)


def softplus(x):
    return jnp.maximum(x, 0.0) + jnp.log1p(jnp.exp(-jnp.abs(x)))


def kernel(low, w_own, rate_own, skip_own, bias_own, sig_hbm, gate_hbm, cot_hbm, seg, c_in, c_out,
           g_sig, g_gate, g_low, g_inc, g_outc, g_w, g_rate, g_skip, g_bias,
           sig, gate, cot, par_own, wall, pall, lowt, seg_s, keep_s, inb, outb, ones, ones32, xs, er,
           dk_s, d_s, ds_s, a_s, r_s, hist, dec_s, y0, y1, q0, q1, z0, z1,
           scan_s, q_s, zz_s, oc_s, ic_s,
           bsend, brecv, bsmall, brsmall, astage, asmall, drecv, srecv, acc, accs, accb, rs, rss, fin,
           w_ss, w_rs, p_ss, p_rs, wf_ss, wf_rs, pf_ss, pf_rs, x_ss, x_rs, b_ss, b_rs, bs_ss, bs_rs,
           d_ss, d_rs, s_ss, s_rs, r_ss, r_rs, t_ss, t_rs, f_ss, f_rs, h_ss, h_rs, seg_ss, seg_rs, own_sem, credit):
    tokens = low.shape[0]
    width = w_own.shape[1]
    states = rate_own.shape[0]
    half = states // 2
    blk = SUB * half
    nblk = tokens // SUB
    seq = lax.axis_index("seq")
    me = lax.axis_index("fsdp")
    chip, core = me // 2, me % 2
    cy, cx = chip // 4, chip % 4
    sibling = (seq, chip * 2 + (1 - core))

    def offset(k):
        late = k // 6
        r = k % 3
        return (1 - late) * (k // 3) + late * (k % 2), (1 - late) * (r + r // 2) + 2 * late

    def device(dy, dx):
        return (seq, (((cy + dy) % 2) * 4 + (cx + dx) % 4) * 2 + core)

    def target(k):
        return device(*offset(k))

    def source_chip(k):
        dy, dx = offset(k)
        return ((cy + dy) % 2) * 4 + (cx + 4 - dx) % 4

    def peer(i):
        return ((seq + i) % 8, me)

    def remote(src, dst, ss, rs_, dev):
        return pltpu.make_async_remote_copy(src_ref=src, dst_ref=dst, send_sem=ss, recv_sem=rs_, device_id=dev, device_id_type=MESH)

    barrier = pltpu.get_barrier_semaphore()
    for k in range(1, PAIRS):
        pl.semaphore_signal(barrier, inc=1, device_id=target(k), device_id_type=MESH)
    for i in range(1, PEERS + 1):
        pl.semaphore_signal(barrier, inc=1, device_id=peer(i), device_id_type=MESH)
    pl.semaphore_signal(barrier, inc=1, device_id=sibling, device_id_type=MESH)
    pl.semaphore_wait(barrier, PAIRS + PEERS)

    def push_p(k):
        return remote(par_own, pall.at[2 * k], p_ss.at[k], p_rs.at[k], target(k))

    def hop(src, k, dev, part=None):
        if part is None:
            return remote(src, wall.at[2 * k], w_ss.at[k], w_rs.at[k], dev)
        rows = pl.ds(part * (w_own.shape[0] // 2), w_own.shape[0] // 2)
        return remote(src.at[rows], wall.at[2 * k, rows], h_ss.at[k - 6, part], h_rs.at[k - 6, part], dev)

    right, left, across = device(0, 1), device(0, 3), device(1, 0)

    def hops(k):
        if k == 1:
            return [hop(w_own, 1, right)]
        if k == 2:
            return [hop(w_own, 2, left)]
        if k == 3:
            return [hop(w_own, 3, across)]
        if k == 4:
            return [hop(wall.at[6], 4, right)]
        if k == 5:
            return [hop(wall.at[6], 5, left)]
        if k == 6:
            return [hop(wall.at[2], 6, right, 0), hop(wall.at[4], 6, left, 1)]
        return [hop(wall.at[8], 7, right, 0), hop(wall.at[10], 7, left, 1)]

    def forward_w(k):
        return (remote(wall.at[2 * k], wall.at[2 * k + 1], wf_ss.at[k], wf_rs.at[k], sibling),
                remote(pall.at[2 * k], pall.at[2 * k + 1], pf_ss.at[k], pf_rs.at[k], sibling))

    def send_seg():
        return remote(seg_s.at[pl.ds(tokens, 8)], seg_s.at[pl.ds(0, 8)], seg_ss, seg_rs, peer(1))

    inputs = [pltpu.make_async_copy(a, b, own_sem.at[2 + i]) for i, (a, b) in enumerate(((sig_hbm, sig), (gate_hbm, gate), (cot_hbm, cot)))]
    for k in (1, 2, 3):
        for c in hops(k):
            c.start()
    own = pltpu.make_async_copy(w_own, wall.at[0], own_sem.at[0])
    own.start()
    for c in inputs:
        c.start()
    par_own[0:states, :] = jnp.maximum(rate_own[...], 1e-30)
    par_own[states:ROWS, :] = jnp.zeros((ROWS - states, width), F32)
    par_own[states:states + 1, :] = skip_own[...]
    par_own[states + 1:states + 2, :] = bias_own[...]
    for k in range(1, PAIRS):
        push_p(k).start()
    ownp = pltpu.make_async_copy(par_own, pall.at[0], own_sem.at[1])
    ownp.start()
    seg_s[8:8 + tokens, :] = jnp.broadcast_to(seg[...].astype(F32), (LANES, tokens)).T
    send_seg().start()
    own.wait()
    ownp.wait()
    for c in forward_w(0):
        c.start()
    for t in range(tokens):
        inb[t * states:(t + 1) * states, :] = jnp.broadcast_to(c_in[:, t:t + 1], (states, LANES))
        outb[t * states:(t + 1) * states, :] = jnp.broadcast_to(c_out[:, t:t + 1], (states, LANES))
    ones[...] = jnp.where(lax.broadcasted_iota(jnp.int32, (SUB, 2 * blk), 1) % blk // half
                          == lax.broadcasted_iota(jnp.int32, (SUB, 2 * blk), 0), 1.0, 0.0).astype(BF16)
    ones32[...] = jnp.where(lax.broadcasted_iota(jnp.int32, (2 * SUB, 2 * blk), 1) // half
                            == lax.broadcasted_iota(jnp.int32, (2 * SUB, 2 * blk), 0), 1.0, 0.0).astype(BF16)
    lowt[...] = low[...].T
    oc_s[...] = jnp.zeros_like(oc_s)
    ic_s[...] = jnp.zeros_like(ic_s)
    g_low[...] = jnp.zeros_like(g_low)
    send_seg().wait_recv()
    keep_s[...] = jnp.where(seg_s[8:8 + tokens, :] == seg_s[7:7 + tokens, :], 1.0, 0.0)
    keep_s[0:1, :] = jnp.where(seq == 0, 0.0, keep_s[0:1, :])
    for c in inputs:
        c.wait()

    def columns(k, other):
        return pl.ds(pl.multiple_of((source_chip(k) * 2 + (core if other == 0 else 1 - core)) * width, width), width)

    def prepare(slot, cols):
        raw = jnp.dot(low[...], wall[slot], preferred_element_type=F32) + pall[slot, states + 1:states + 2, :]
        delta = softplus(raw)
        g = gate[:, cols].astype(F32)
        a = cot[:, cols].astype(F32) * g * jax.nn.sigmoid(g)
        dk_s[...] = jnp.where(wide(keep_s[...], width) > 0, delta, jnp.inf)
        ds = delta * sig[:, cols].astype(F32)
        ds_s[...] = ds
        a_s[...] = a
        return raw, delta, ds, a

    def rates(slot):
        return pall[slot, 0:states, :] * (-LOG2E)

    def block(i):
        return pl.ds(pl.multiple_of(i * SUB, SUB), SUB)

    def coef(ref, t):
        return wide(ref[pl.ds(pl.multiple_of(t * states, states), states), :], width)

    def local_pass(slot, cols, up, down, second):
        prepare(slot, cols)
        nrate = rates(slot)

        def body(i, carry):
            st, ad = carry
            for u in range(SUB):
                t = i * SUB + u
                d1 = dk_s.at[block(i), :]
                d2 = dk_s.at[block(nblk - 1 - i), :]
                v = SUB - 1 - u
                st = jnp.exp2(nrate * d1[u:u + 1, :]) * st + coef(inb, t) * ds_s.at[block(i), :][u:u + 1, :]
                ad = jnp.exp2(nrate * d2[v:v + 1, :]) * (coef(outb, tokens - 1 - t) * a_s.at[block(nblk - 1 - i), :][v:v + 1, :] + ad)
            return st, ad
        zero = jnp.zeros((states, width), F32)
        st, ad = lax.fori_loop(0, nblk, body, (zero, zero))
        total = jnp.sum(dk_s[...], 0, keepdims=True)
        at = pl.ds(second * states, states)
        last = ENDS - 2 * states if not second else 1
        total = jnp.broadcast_to(total, (last, width))
        up[at, :] = st
        down[at, :] = ad
        up[2 * states + second:2 * states + second + last, :] = total
        down[2 * states + second:2 * states + second + last, :] = total

    def send_ends(k, i):
        return remote(xs.at[k, (seq + i) // 8], er.at[k, i - 1], x_ss.at[k, i - 1], x_rs.at[k, i - 1], peer(i))

    def shared(k):
        for c in forward_w(k):
            c.start()

    def came(k):
        for c in hops(k):
            c.wait_recv()
        push_p(k).wait_recv()

    def first(k, carry):
        @pl.when(k == 1)
        def _():
            for j in (1, 2, 3):
                came(j)
            for j in (4, 5, 6):
                for c in hops(j):
                    c.start()
            for j in (1, 2, 3):
                shared(j)

        @pl.when(k == 4)
        def _():
            for j in (4, 5):
                came(j)
            for c in hops(7):
                c.start()
            for j in (4, 5):
                shared(j)

        @pl.when(k == 6)
        def _():
            came(6)
            shared(6)

        @pl.when(k == 7)
        def _():
            came(7)
            shared(7)
        local_pass(2 * k, columns(k, 0), xs.at[k, 0], xs.at[k, 1], 0)
        for c in forward_w(k):
            c.wait_recv()
        local_pass(2 * k + 1, columns(k, 1), xs.at[k, 0], xs.at[k, 1], 1)
        for i in range(1, PEERS + 1):
            send_ends(k, i).start()
        return carry
    lax.fori_loop(0, PAIRS, first, 0)

    def entering(k, base, nrate):
        total = 2 * states + base // states
        st = jnp.zeros((states, width), F32)
        ad = jnp.zeros((states, width), F32)
        for i in range(PEERS, 0, -1):
            e = er.at[k, i - 1]
            st = jnp.where(seq >= i, jnp.exp2(nrate * e[total:total + 1, :]) * st + e[base:base + states, :], st)
            e = er.at[k, PEERS - i]
            ad = jnp.where(seq + i < 8, jnp.exp2(nrate * e[total:total + 1, :]) * ad + e[base:base + states, :], ad)
        return st, ad

    def folded(x):
        return x[:half] + x[half:]

    def lane_groups(x):
        return functools.reduce(lambda p, q: p + q, [x[:, g * LANES:(g + 1) * LANES] for g in range(width // LANES)])

    def ones_dot(m, x):
        return jnp.dot(m[...], x[...], preferred_element_type=F32)

    def full_pass(k, slot, cols, base, small):
        raw, delta, ds, a = prepare(slot, cols)
        d_s[...] = delta
        r_s[...] = jax.nn.sigmoid(raw)
        nrate = rates(slot)
        st0, ad0 = entering(k, base, nrate)
        hist[0:states, :] = st0

        def fwd_vec(b, st, y, off):
            held = None
            for u in range(SUB):
                row = pl.multiple_of((b * SUB + u) * states, states)
                here = pl.ds(row, states)
                dec = jnp.exp2(nrate * dk_s.at[block(b), :][u:u + 1, :])
                dec_s[here, :] = dec
                st = dec * st + coef(inb, b * SUB + u) * ds_s.at[block(b), :][u:u + 1, :]
                hist[pl.ds(row + states, states), :] = st
                oc_s[here, :] += lane_groups(st * a_s.at[block(b), :][u:u + 1, :])
                part = folded(st * coef(outb, b * SUB + u))
                if u % 2:
                    y[off + (u - 1) * half:off + (u + 1) * half, :] = jnp.concatenate([held, part], 0).astype(BF16)
                held = part
            return st

        def rows(b, size):
            return pl.ds(pl.multiple_of((b + 1) * size, size), size)

        def fwd_mat(b, y):
            scan_s[rows(b, 2 * SUB), :] = ones_dot(ones32, y)

        def fwd(i, st):
            st = fwd_vec(4 * i, st, y0, 0)
            fwd_mat(2 * i - 1, y1)
            st = fwd_vec(4 * i + 1, st, y0, blk)
            st = fwd_vec(4 * i + 2, st, y1, 0)
            fwd_mat(2 * i, y0)
            return fwd_vec(4 * i + 3, st, y1, blk)
        lax.fori_loop(0, nblk // 4, fwd, st0)
        fwd_mat(nblk // 2 - 1, y1)

        def bwd_vec(b, ca, rg, qb, zb, off):
            held = None
            for u in reversed(range(SUB)):
                row = pl.multiple_of((b * SUB + u) * states, states)
                here = pl.ds(row, states)
                adj = coef(outb, b * SUB + u) * a_s.at[block(b), :][u:u + 1, :] + ca
                ic_s[here, :] += lane_groups(adj * ds_s.at[block(b), :][u:u + 1, :])
                ca = dec_s[here, :] * adj
                z = ca * hist[here, :]
                rg = rg + z * d_s.at[block(b), :][u:u + 1, :]
                part = folded(adj * coef(inb, b * SUB + u)), folded(z * nrate)
                if u % 2 == 0:
                    at = slice(u * half, (u + 2) * half)
                    pair = jnp.concatenate([part[0], held[0]], 0)
                    hi = pair.astype(BF16)
                    qb[at, :] = hi
                    qb[blk + u * half:blk + (u + 2) * half, :] = (pair - hi.astype(F32)).astype(BF16)
                    zb[off + u * half:off + (u + 2) * half, :] = jnp.concatenate([part[1], held[1]], 0).astype(BF16)
                held = part
            return ca, rg

        def q_mat(b, qb):
            q_s[rows(b, SUB), :] = ones_dot(ones, qb)

        def z_mat(b, zb):
            zz_s[rows(b, 2 * SUB), :] = ones_dot(ones32, zb)

        def bwd(i, carry):
            b = nblk - 1 - 4 * i
            g = nblk // 2 - 1 - 2 * i
            carry = bwd_vec(b, *carry, q0, z0, blk)
            q_mat(b + 1, q1)
            z_mat(g + 1, z1)
            carry = bwd_vec(b - 1, *carry, q1, z0, 0)
            q_mat(b, q0)
            carry = bwd_vec(b - 2, *carry, q0, z1, blk)
            q_mat(b - 1, q1)
            z_mat(g, z0)
            carry = bwd_vec(b - 3, *carry, q1, z1, 0)
            q_mat(b - 2, q0)
            return carry
        _, rg = lax.fori_loop(0, nblk // 4, bwd, (ad0, jnp.zeros((states, width), F32)))
        q_mat(0, q1)
        z_mat(0, z1)

        q = q_s[SUB:SUB + tokens, :]
        s = sig[:, cols].astype(F32)
        g = gate[:, cols].astype(F32)
        o = cot[:, cols].astype(F32)
        sg = jax.nn.sigmoid(g)
        av = a_s[...]
        gain = pall[slot, states:states + 1, :]
        g_gate[:, cols] = (o * (scan_s[2 * SUB:2 * SUB + tokens, :] + gain * s) * sg * (1.0 + g * (1.0 - sg))).astype(BF16)
        g_sig[:, cols] = (d_s[...] * q + gain * av).astype(BF16)
        rawg = (s * q + zz_s[2 * SUB:2 * SUB + tokens, :] * (1.0 / LOG2E)) * r_s[...]
        small[0:states, :] = -rg
        small[states:ROWS, :] = jnp.zeros((ROWS - states, width), F32)
        small[states:states + 1, :] = jnp.sum(s * av, 0, keepdims=True)
        small[states + 1:states + 2, :] = jnp.sum(rawg, 0, keepdims=True)
        rr = rawg.astype(BF16)
        g_low[...] += nt(rr, wall[slot])
        return jnp.dot(lowt[...], rr, preferred_element_type=F32)

    def to_sibling(k):
        return (remote(bsend.at[k % 2], brecv.at[k % 2], b_ss.at[k], b_rs.at[k], sibling),
                remote(bsmall.at[k % 2], brsmall.at[k % 2], bs_ss.at[k], bs_rs.at[k], sibling))

    def to_owner(k):
        dev = (seq, source_chip(k) * 2 + core)
        return (remote(astage.at[k % 2], drecv.at[k - 1], d_ss.at[k], d_rs.at[k], dev),
                remote(asmall.at[k % 2], srecv.at[k - 1], s_ss.at[k], s_rs.at[k], dev))

    def second(m, carry):
        k = (m + 1) % PAIRS
        for i in range(1, PEERS + 1):
            send_ends(k, i).wait_recv()

        @pl.when(m >= 2)
        def _():
            for c in to_sibling(m - 1):
                c.wait_send()
            pl.semaphore_wait(credit, 1)
        bsend[k % 2] = full_pass(k, 2 * k + 1, columns(k, 1), states, bsmall.at[k % 2])
        for c in to_sibling(k):
            c.start()

        @pl.when((m >= 2) & (m < PAIRS - 1))
        def _():
            for c in to_owner(m - 1):
                c.wait_send()
        acc[...] = full_pass(k, 2 * k, columns(k, 0), 0, accs)
        for c in to_sibling(k):
            c.wait_recv()
        acc[...] += brecv[k % 2]
        accs[...] += brsmall[k % 2]

        @pl.when(m < PAIRS - 2)
        def _():
            pl.semaphore_signal(credit, inc=1, device_id=sibling, device_id_type=MESH)

        @pl.when(m < PAIRS - 1)
        def _():
            astage[k % 2] = acc[...].astype(BF16)
            asmall[k % 2] = accs[...]
            for c in to_owner(k):
                c.start()
        return carry
    lax.fori_loop(0, PAIRS, second, 0)

    def add_in(k, carry):
        for c in to_owner(k):
            c.wait_recv()
        acc[...] += drecv[k - 1].astype(F32)
        accs[...] += srecv[k - 1]
        return carry
    lax.fori_loop(1, PAIRS, add_in, 0)

    rank = acc.shape[0]
    part = rank // 8

    def part_of(i):
        return pl.ds(pl.multiple_of(((seq + i) % 8) * part, part), part)

    def scatter(i):
        return (remote(accb.at[part_of(i)], rs.at[seq], r_ss.at[i - 1], r_rs.at[i - 1], peer(i)),
                remote(accs, rss.at[seq], t_ss.at[i - 1], t_rs.at[i - 1], peer(i)))

    def arrived(i):
        j = (seq + 8 - i) % 8
        return (remote(accb.at[part_of(0)], rs.at[j], r_ss.at[i - 1], r_rs.at[i - 1], peer(i)),
                remote(accs, rss.at[j], t_ss.at[i - 1], t_rs.at[i - 1], peer(i)))

    def gather(i):
        return remote(fin.at[part_of(0)], fin.at[part_of(0)], f_ss.at[i - 1], f_rs.at[i - 1], peer(i))

    def gathered(i):
        return remote(fin.at[part_of(8 - i)], fin.at[part_of(8 - i)], f_ss.at[i - 1], f_rs.at[i - 1], peer(i))

    accb[...] = acc[...].astype(BF16)
    for i in range(1, PEERS + 1):
        for c in scatter(i):
            c.start()
    rs[seq] = accb[part_of(0), :]
    rss[seq] = accs[...]
    for i in range(1, PEERS + 1):
        for c in arrived(i):
            c.wait_recv()
    total, small = rs[0].astype(F32), rss[0]
    for i in range(1, PEERS + 1):
        total = total + rs[i].astype(F32)
        small = small + rss[i]
    fin[part_of(0), :] = total
    g_rate[...] = small[0:states]
    g_skip[...] = small[states:states + 1]
    g_bias[...] = small[states + 1:states + 2]
    for i in range(1, PEERS + 1):
        gather(i).start()

    for src, dst in ((oc_s, g_outc), (ic_s, g_inc)):
        for n in range(states):
            dst[n:n + 1, :] = jnp.sum(src[pl.ds(n, tokens, stride=states), :].T, 0, keepdims=True)

    for i in range(1, PEERS + 1):
        gathered(i).wait_recv()
    g_w[...] = fin[...]

    send_seg().wait_send()
    for k in range(PAIRS):
        for c in forward_w(k):
            c.wait_send()
        for i in range(1, PEERS + 1):
            send_ends(k, i).wait_send()
    for k in range(1, PAIRS):
        for c in hops(k):
            c.wait_send()
        push_p(k).wait_send()
    for k in (PAIRS - 1, 0):
        for c in to_sibling(k):
            c.wait_send()
    for k in (PAIRS - 2, PAIRS - 1):
        for c in to_owner(k):
            c.wait_send()
    for i in range(1, PEERS + 1):
        for c in scatter(i):
            c.wait_send()
        gather(i).wait_send()


def run(low, w, rate, skip, bias, sig, gate, cot, seg, c_in, c_out):
    tokens, chans = sig.shape
    rank, width = w.shape
    n = rate.shape[0]
    blk = SUB * n // 2
    rows16 = (tokens // SUB + 2) * SUB
    S = jax.ShapeDtypeStruct
    vm = lambda *shape: pltpu.VMEM(shape, F32)
    vb = lambda *shape: pltpu.VMEM(shape, BF16)
    dma = lambda *shape: pltpu.SemaphoreType.DMA(shape)
    scratch = [vb(tokens, chans)] * 3 + [
        vm(ROWS, width), vb(16, rank, width), vm(16, ROWS, width), vb(rank, tokens), vm(tokens + 8, LANES), vm(tokens, LANES),
        vm(tokens * n, LANES), vm(tokens * n, LANES), vb(SUB, 2 * blk), vb(2 * SUB, 2 * blk),
        vm(PAIRS, 2, ENDS, width), vm(PAIRS, PEERS, ENDS, width),
    ] + [vm(tokens, width)] * 5 + [vm((tokens + 1) * n, width), vm(tokens * n, width)] + [
        ] + [vb(2 * blk, width)] * 6 + [
        vm(rows16 + 2 * SUB, width), vm(rows16, width), vm(rows16 + 2 * SUB, width), vm(tokens * n, LANES), vm(tokens * n, LANES),
        vm(2, rank, width), vm(2, rank, width), vm(2, ROWS, width), vm(2, ROWS, width),
        vb(2, rank, width), vm(2, ROWS, width), vb(PAIRS - 1, rank, width), vm(PAIRS - 1, ROWS, width),
        vm(rank, width), vm(ROWS, width), vb(rank, width), vb(8, rank // 8, width), vm(8, ROWS, width), vm(rank, width),
    ] + [dma(PAIRS)] * 8 + [dma(PAIRS, PEERS)] * 2 + [dma(PAIRS)] * 8 + [dma(PEERS)] * 6 + [dma(2, 2)] * 2 + [
        pltpu.SemaphoreType.DMA, pltpu.SemaphoreType.DMA, dma(5), pltpu.SemaphoreType.REGULAR]
    points = tokens * n * chans
    vmem, hbm = pl.BlockSpec(memory_space=pltpu.VMEM), pl.BlockSpec(memory_space=pl.ANY)
    return pl.pallas_call(
        kernel,
        in_specs=[vmem] * 5 + [hbm] * 3 + [vmem] * 3,
        out_specs=[vmem] * 9,
        out_shape=[S((tokens, chans), BF16), S((tokens, chans), BF16), S((tokens, rank), F32), S((n, tokens), F32),
                   S((n, tokens), F32), S((rank, width), F32), S((n, width), F32), S((1, width), F32), S((1, width), F32)],
        scratch_shapes=scratch,
        cost_estimate=pl.CostEstimate(flops=30 * points, bytes_accessed=20 << 20, transcendentals=3 * points),
        compiler_params=pltpu.CompilerParams(vmem_limit_bytes=63 << 20, collective_id=0, has_side_effects=True),
        name="scan_backward",
    )(low, w, rate, skip, bias, sig, gate, cot, seg, c_in, c_out)


def shards(signal, gating, low_rank, dt_weight, dt_bias, decay_rate, skip_gain, coef_in, coef_out, segment_ids, out_grad):
    g_sig, g_gate, g_low, g_inc, g_outc, g_w, g_rate, g_skip, g_bias = run(
        low_rank[0], dt_weight, decay_rate, skip_gain[None], dt_bias[None], signal[0], gating[0], out_grad[0],
        segment_ids, coef_in[0], coef_out[0])
    return (g_sig[None], g_gate[None], g_low[None], g_inc[None], g_outc[None], g_w, g_rate, g_skip[0], g_bias[0])


def solution(mesh):
    return jax.shard_map(
        shards,
        mesh=mesh,
        in_specs=(
            P("fsdp", "seq", None), P("fsdp", "seq", None), P("fsdp", "seq", None),
            P(None, "fsdp"), P("fsdp"), P(None, "fsdp"), P("fsdp"),
            P("fsdp", None, "seq"), P("fsdp", None, "seq"), P("fsdp", "seq"), P("fsdp", "seq", None),
        ),
        out_specs=(
            P("fsdp", "seq", None), P("fsdp", "seq", None), P("fsdp", "seq", None),
            P("fsdp", None, "seq"), P("fsdp", None, "seq"), P(None, "fsdp"), P(None, "fsdp"), P("fsdp"), P("fsdp"),
        ),
        check_vma=False,
    )
```
